768 devices in a mesh: dp: 16 (over y, core), expert: 48 (over z, x).
Axes of the slice: x: 4, y: 8, z: 12, core: 2. Of those that a mesh axis runs over, the one named last changes fastest.
Arguments:
- hidden_in: bfloat16 [48, 128, 4096], P('expert', None, 'dp'), may hold values from -6 to 6
- out_grad: bfloat16 [48, 128, 4096], P('expert', None, 'dp'), may hold values from -6 to 6
- routes: int32 [48, 128, 8], P('expert'), may hold values from 0 to 95, all different within a row; in each aligned block of 128 rows (0 to 127, 128 to 255, ..., all dimensions but the last counted through in order) at most 11 rows name the same one
- router_weight: bfloat16 [4096, 96], P('dp'), may hold values from -0.09375 to 0.09375
- expert_bias: float32 [96], replicated, may hold values from -1 to 1
- gate_weight: bfloat16 [96, 4096, 768], P('expert', 'dp'), may hold values from -0.09375 to 0.09375
- up_weight: bfloat16 [96, 4096, 768], P('expert', 'dp'), may hold values from -0.09375 to 0.09375
- down_weight: bfloat16 [96, 768, 4096], P('expert', None, 'dp'), may hold values from -0.21875 to 0.21875
- lengths: int32 [48, 8], P('expert'), may hold values from 1 to 32, 128 in all within a row
- advantages: float32 [48, 8], P('expert'), may hold values from -4 to 4
- plan: int32 [48, 8], P('expert'), may hold values from 0 to 11, as said below
Outputs:
- layer_out: bfloat16 [48, 128, 4096], P('expert', None, 'dp')
- input_grad: bfloat16 [48, 128, 4096], P('expert', None, 'dp')
- new_bias: float32 [96], replicated
The draws below stay inside these ranges and needn't reach their ends.
Inputs may be any that keep to these rules, and one draw needn't show every extreme that they name: `routes`: each row names 8 different experts. In each aligned block of 128 rows (the tokens of one column) no expert is named by more than 11 rows, a bound that some block reaches. `plan`: every learner group holds at least one response.
All inputs are finite; a program needn't handle non-finite values.
Results may differ from the reference program's by a relative error of at most 0.04.
Values may be sent and summed in bfloat16 or wider, within the bound.
No kernel may reach another device: no remote copies, remote signals or barrier semaphores. Data moves between devices by JAX's collectives and lax.ppermute only.
A program may use at most 64 MiB of HBM per device.

```python
import math
import jax
import jax.numpy as jnp
import numpy as np
from jax import lax

D = 4096
FF = 768
EXPERTS = 96
TOPK = 8
COL_TOK = 128
MOSTE = 11
RESP_COL = 8
L_MOST = 32
LEARN_GROUPS = 12
RESPONSES = 384
N_DP = 16
N_EXPERT = 48


def draw_plan(key, part):
    key = jax.random.fold_in(key, 11)
    first_key, second_key = jax.random.split(key)
    order = jax.random.permutation(first_key, RESPONSES)
    ranking = jnp.argsort(order)
    random_groups = jax.random.randint(second_key, (RESPONSES,), 0, LEARN_GROUPS)
    chosen = jnp.where(ranking < LEARN_GROUPS, ranking, random_groups)
    return chosen.astype(jnp.int32).reshape(RESPONSES // RESP_COL, RESP_COL)


def levels(stream_key, shape, shards, smallest, high):
    factor_of = 1.0
    for dim, blocks in shards:
        heights = jax.random.uniform(jax.random.fold_in(jax.random.fold_in(stream_key, 6), dim), (blocks,), jnp.float32, smallest / len(shards), high / len(shards))
        factor_of = factor_of * jnp.repeat(jnp.exp(heights), shape[dim] // blocks).reshape((-1,) + (1,) * (len(shape) - 1 - dim))
    return factor_of


def profile(amount, total, reach, skew):
    weights = [(1 << 20) // math.isqrt(rank ** skew) + 1 for rank in range(2, amount + 1)]
    spare, counts = total - reach - (amount - 1), [1] * (amount - 1)
    while spare > 0:
        free = [i for i in range(amount - 1) if counts[i] < reach]
        whole, left = sum([weights[i] for i in free]), spare
        for i in free:
            addition = min(reach - counts[i], max(1, left * weights[i] // whole), spare)
            counts[i] = counts[i] + addition
            spare = spare - addition
    return np.array([reach] + counts)


def uneven(stream_key, amount, total, most, skew):
    if amount == 2:
        one = jax.random.randint(stream_key, (), max(1, total - most), min(most, total - 1) + 1)
        return jnp.stack([one, total - one])
    tallies = jnp.asarray(profile(amount, total, most, skew), jnp.int32)
    twos = (amount - 1) // 2
    giver, receiver = tallies[1:1 + 2 * twos:2], tallies[2:2 + 2 * twos:2]
    room = jnp.minimum(giver - 1, most - receiver)
    passed = jax.random.randint(jax.random.fold_in(stream_key, 1), (twos,), 0, 1 << 20) % (room + 1)
    tallies = tallies.at[1:1 + 2 * twos:2].set(giver - passed).at[2:2 + 2 * twos:2].set(receiver + passed)
    return tallies[jax.random.permutation(jax.random.fold_in(stream_key, 2), amount)]


def assign_block(own_key, own, number, rows, count, top, reach, skew):
    sequence = jax.random.permutation(own_key, count)
    crowded, ordinary = shares(count, rows * top, reach, skew, True), shares(count, rows * top, reach, skew, False)
    places = jnp.arange(count)

    def named(sizes, offset_by):
        used = int((sizes > 0).sum())
        fixed = max(1, used // 4)
        passed = fixed + (places - fixed + offset_by * (used - fixed)) % max(1, count - fixed)
        return jnp.zeros((count,), jnp.int32).at[sequence[jnp.where(places < fixed, places, passed)]].set(jnp.asarray(sizes, jnp.int32))

    sizes = jnp.where(number % 4 == 0, named(crowded, number // 4), named(ordinary, number - number // 4 - 1))
    mixed = jax.random.permutation(jax.random.fold_in(own, 3), count)
    source_of, receiver = mixed[0:count // 2 * 2:2], mixed[1:count // 2 * 2:2]
    slack = jnp.minimum(sizes[source_of] - 1, reach - sizes[receiver]) // 2
    slack = jnp.where((source_of == sequence[0]) | (receiver == sequence[0]) | (sizes[receiver] == 0), 0, jnp.maximum(slack, 0))
    passed = jax.random.randint(jax.random.fold_in(own, 4), (count // 2,), 0, 1 << 20) % (slack + 1)
    sizes = sizes.at[source_of].add(-passed).at[receiver].add(passed)
    members = jnp.searchsorted(jnp.cumsum(sizes), jnp.arange(rows * top), side="right").astype(jnp.int32)
    listing = members.reshape(top, rows).T
    listing = listing[jax.random.permutation(jax.random.fold_in(own, 1), rows)]
    offset_by = jax.random.randint(jax.random.fold_in(own, 2), (rows, 1), 0, top)
    return jnp.take_along_axis(listing, (jnp.arange(top)[None, :] + offset_by) % top, axis=1)


def shares(count, total, limit, skew, full):
    loads = [(1 << 20) // math.isqrt(standing ** skew) + 1 for standing in range(1, count + 1)]
    largest = limit if full else min(limit, max(-(-total // count), total * loads[0] // sum(loads)))
    least = 1 if total - largest >= count - 1 else 0
    given, spare = [largest] + [least] * (count - 1), total - largest - least * (count - 1)
    while spare > 0:
        movable = [i for i in range(1, count) if given[i] < largest] or [i for i in range(1, count) if given[i] < limit]
        mass, left = sum([loads[i] for i in movable]), spare
        for i in movable:
            addition = min(limit - given[i], max(1, left * loads[i] // mass), spare)
            given[i] = given[i] + addition
            spare = spare - addition
    return np.array(given)


def scatter_about(key, shape, width, limit, pieces=(), kind=jnp.bfloat16):
    drawn = jax.random.normal(key, shape, jnp.float32) * width
    if len(pieces) > 0:
        drawn = levels(key, shape, pieces, -0.22, 0.18) * drawn
    return jnp.clip(drawn, min=-limit, max=limit).astype(kind)


def setup_inputs(seed: int = 0) -> dict:
    key_list = jax.random.split(jax.random.key(seed), 12)
    hidden_in = scatter_about(key_list[0], (N_EXPERT, COL_TOK, D), 1.0, 6.0, ((0, 48), (2, 16)))
    out_grad = scatter_about(key_list[1], (N_EXPERT, COL_TOK, D), 1.0, 6.0, ((0, 48), (2, 16)))
    routes_keys = jax.random.split(jax.random.fold_in(key_list[2], 1), N_EXPERT * COL_TOK // COL_TOK)
    routes_turns = jax.random.permutation(jax.random.fold_in(key_list[2], 3), N_EXPERT * COL_TOK // COL_TOK)
    routes = jax.vmap(lambda own, number: assign_block(jax.random.fold_in(key_list[2], 2), own, number, COL_TOK, EXPERTS, TOPK, MOSTE, 2))(routes_keys, routes_turns).reshape((N_EXPERT, COL_TOK, TOPK))
    router_weight = scatter_about(key_list[3], (D, EXPERTS), D ** -0.5, 0.09375, ((0, 16),))
    expert_bias = jnp.clip(jax.random.uniform(key_list[4], (EXPERTS,), jnp.float32, -1.0, 1.0), -1.0, 1.0)
    gate_weight = scatter_about(key_list[5], (EXPERTS, D, FF), D ** -0.5, 0.09375, ((0, 48), (1, 16)))
    up_weight = scatter_about(key_list[6], (EXPERTS, D, FF), D ** -0.5, 0.09375, ((0, 48), (1, 16)))
    down_weight = scatter_about(key_list[7], (EXPERTS, FF, D), FF ** -0.5, 0.21875, ((0, 48), (2, 16)))
    lengths = jax.vmap(lambda own: uneven(own, RESP_COL, COL_TOK, L_MOST, 2))(jax.random.split(key_list[8], N_EXPERT)).reshape((N_EXPERT, RESP_COL)).astype(jnp.int32)
    advantages = scatter_about(key_list[9], (N_EXPERT, RESP_COL), 1.0, 4.0, ((0, 48),), jnp.float32)
    plan = draw_plan(jax.random.fold_in(key_list[11], 71), 0)
    return {"hidden_in": hidden_in, "out_grad": out_grad, "routes": routes, "router_weight": router_weight, "expert_bias": expert_bias, "gate_weight": gate_weight, "up_weight": up_weight, "down_weight": down_weight, "lengths": lengths, "advantages": advantages, "plan": plan}


bias_rate = 0.1


def reference(hidden_in, out_grad, routes, router_weight, expert_bias, gate_weight, up_weight, down_weight, lengths, advantages, plan):
    columns, column_rows, model_width = hidden_in.shape
    experts = router_weight.shape[1]
    top_count = routes.shape[2]
    hidden_units = gate_weight.shape[2]
    token_total = columns * column_rows
    part_width = model_width // N_DP
    capacity = column_rows * top_count // experts + 1
    tokens = hidden_in.reshape(token_total, model_width)
    cotangents = out_grad.reshape(token_total, model_width)
    flat_routes = routes.reshape(token_total, top_count)
    scores = jax.nn.sigmoid(jnp.dot(tokens, router_weight, preferred_element_type=jnp.float32))
    chosen = jnp.take_along_axis(scores, flat_routes, axis=1)
    mixing = (chosen / jnp.sum(chosen, axis=1, keepdims=True)).astype(jnp.bfloat16)
    column_routes = routes.reshape(columns, column_rows * top_count)
    member = (column_routes[:, :, None] == jnp.arange(experts, dtype=jnp.int32)[None, None, :]).astype(jnp.int32)
    position = jnp.sum((jnp.cumsum(member, axis=1) - member) * member, axis=2).astype(jnp.int32)
    expert_loads = jnp.sum(member, axis=(0, 1)).astype(jnp.float32)
    column_index = jnp.broadcast_to(jnp.arange(columns, dtype=jnp.int32)[:, None], column_routes.shape)
    token_index = (column_index * column_rows + jnp.arange(column_rows * top_count, dtype=jnp.int32)[None, :] // top_count).astype(jnp.int32)
    slot_table = jnp.full((experts, columns, capacity), -1, jnp.int32).at[column_routes, column_index, position].set(token_index)
    weight_table = jnp.zeros((experts, columns, capacity), jnp.float32).at[column_routes, column_index, position].set(
        mixing.reshape(columns, column_rows * top_count).astype(jnp.float32))

    def settle(partial_value):
        rounded = lax.optimization_barrier(partial_value.astype(jnp.bfloat16))
        return jnp.sum(rounded.astype(jnp.float32), axis=1)

    def one_expert(running, inputs):
        out_sum, in_sum = running
        indices, weight, gate_w, up_w, down_w = inputs
        indices = indices.reshape(-1)
        weight = weight.reshape(-1)
        filled = indices >= 0
        safe_index = jnp.maximum(indices, 0)
        slot_count = indices.shape[0]
        expert_x = jnp.where(filled[:, None], tokens[safe_index], jnp.zeros((), jnp.bfloat16))
        expert_grad = jnp.where(filled[:, None], weight[:, None] * cotangents[safe_index].astype(jnp.float32), 0.0).astype(jnp.bfloat16)
        blocks_x = expert_x.reshape(slot_count, N_DP, part_width).astype(jnp.float32)
        blocks_grad = expert_grad.reshape(slot_count, N_DP, part_width).astype(jnp.float32)
        gate_blocks = gate_w.reshape(N_DP, part_width, hidden_units).astype(jnp.float32)
        up_blocks = up_w.reshape(N_DP, part_width, hidden_units).astype(jnp.float32)
        down_blocks = down_w.reshape(hidden_units, N_DP, part_width).astype(jnp.float32)
        gate_part = settle(jnp.einsum("rbd,bdf->rbf", blocks_x, gate_blocks))
        up_part = settle(jnp.einsum("rbd,bdf->rbf", blocks_x, up_blocks))
        backward = settle(jnp.einsum("rbd,fbd->rbf", blocks_grad, down_blocks))
        sigmoid_gate = jax.nn.sigmoid(gate_part)
        swish_gate = gate_part * sigmoid_gate
        hidden = (swish_gate * up_part).astype(jnp.bfloat16)
        grad_gate = (backward * up_part * sigmoid_gate * (1.0 + gate_part * (1.0 - sigmoid_gate))).astype(jnp.bfloat16)
        grad_up = (backward * swish_gate).astype(jnp.bfloat16)
        output = jnp.dot(hidden, down_w, preferred_element_type=jnp.float32).astype(jnp.bfloat16)
        input_part = (jnp.dot(grad_gate, gate_w.T, preferred_element_type=jnp.float32)
                      + jnp.dot(grad_up, up_w.T, preferred_element_type=jnp.float32)).astype(jnp.bfloat16)
        out_sum = out_sum.at[safe_index].add(jnp.where(filled[:, None], weight[:, None] * output.astype(jnp.float32), 0.0))
        in_sum = in_sum.at[safe_index].add(jnp.where(filled[:, None], input_part.astype(jnp.float32), 0.0))
        return (out_sum, in_sum), None

    empty = jnp.zeros((token_total, model_width), jnp.float32)
    (out_sum, in_sum), _ = lax.scan(one_expert, (empty, empty), (slot_table, weight_table, gate_weight, up_weight, down_weight))
    resp_ends = jnp.cumsum(lengths, axis=1)
    token_resp = jnp.sum((jnp.arange(column_rows, dtype=jnp.int32)[None, :, None] >= resp_ends[:, None, :]).astype(jnp.int32), axis=2)
    token_adv = jnp.take_along_axis(advantages, token_resp, axis=1).reshape(token_total)
    token_plan = jnp.take_along_axis(plan, token_resp, axis=1).reshape(token_total)
    group_hot = plan.reshape(-1)[:, None] == jnp.arange(LEARN_GROUPS, dtype=jnp.int32)[None, :]
    group_tokens = jnp.sum(jnp.where(group_hot, lengths.reshape(-1)[:, None], 0), axis=0).astype(jnp.float32)
    token_scale = token_adv * (token_total / LEARN_GROUPS) / group_tokens[token_plan]
    layer_out = out_sum.astype(jnp.bfloat16).reshape(columns, column_rows, model_width)
    input_grad = (token_scale[:, None] * in_sum).astype(jnp.bfloat16).reshape(columns, column_rows, model_width)
    new_bias = expert_bias + bias_rate * (1.0 - expert_loads / (token_total * top_count / experts))
    return layer_out, input_grad, new_bias
```

```python
import jax
import jax.numpy as jnp
import numpy as np
from jax import lax
from jax.experimental import pallas as pl
from jax.experimental.pallas import tpu as pltpu
from jax.sharding import Mesh, PartitionSpec as P

LEARN_GROUPS = 12
bias_rate = 0.1
BF = jnp.bfloat16
F32 = jnp.float32


def nn(a, b):
    return lax.dot_general(a, b, (((1,), (0,)), ((), ())), preferred_element_type=F32)


def nt(a, b):
    return lax.dot_general(a, b, (((1,), (1,)), ((), ())), preferred_element_type=F32)


def ranks(routes_t, experts):
    tops, rows = routes_t.shape
    ids = lax.broadcasted_iota(jnp.int32, (experts, rows), 0)
    member = ids == routes_t[0:1, :]
    for k in range(1, tops):
        member = member | (ids == routes_t[k : k + 1, :])
    hot = member.astype(F32).astype(BF)
    earlier = (
        lax.broadcasted_iota(jnp.int32, (rows, rows), 0) < lax.broadcasted_iota(jnp.int32, (rows, rows), 1)
    ).astype(F32).astype(BF)
    place = nn(hot, earlier)
    return hot, jnp.where(member, place, -1.0).astype(BF)


def dispatch_kernel(room, routes_ref, lens_ref, plan_ref, x_ref, g_ref, buf_ref):
    experts = buf_ref.shape[0] // room
    total = buf_ref.shape[0]
    rows, width = x_ref.shape
    hot, value = ranks(routes_ref[...], experts)
    row = lax.broadcasted_iota(jnp.int32, (total, experts), 0)
    first = lax.broadcasted_iota(jnp.int32, (total, experts), 1) * room
    spread = ((row >= first) & (row < first + room)).astype(F32).astype(BF)
    wide = nn(spread, value)
    line = lax.broadcasted_iota(jnp.int32, (total, rows), 0)
    select = (wide.astype(jnp.int32) == lax.rem(line, room)).astype(F32).astype(BF)
    loads = nt(jnp.ones((8, rows), BF), hot)[0:1, :]
    group = lax.broadcasted_iota(jnp.int32, (1, width // 2), 1)
    chosen = jnp.zeros((1, width // 2), F32)
    for r in range(plan_ref.shape[1]):
        chosen = chosen + jnp.where(group == plan_ref[0, r], lens_ref[0, r], 0).astype(F32)
    pad = jnp.zeros((1, width // 2 - experts), F32)
    counts = jnp.concatenate([loads, pad, chosen], axis=1)
    carrier = lax.rem(lax.broadcasted_iota(jnp.int32, (total, width), 0), 2 * room) == room - 1
    sent = nn(select, x_ref[...])
    buf_ref[:, :width] = jnp.where(carrier, jnp.broadcast_to(counts, sent.shape), sent).astype(BF)
    buf_ref[:, width:] = nn(select, g_ref[...]).astype(BF)


def expand_kernel(room, own_ref, oth_ref, go_ref, gx_ref, uo_ref, ux_ref, do_ref, dx_ref, out_ref):
    rows = own_ref.shape[0]
    width = own_ref.shape[1] // 2
    tile = go_ref.shape[2]
    own_x, own_g = own_ref[:, :width], own_ref[:, width:]
    oth_x, oth_g = oth_ref[:, :width], oth_ref[:, width:]
    first = lax.rem(lax.broadcasted_iota(jnp.int32, (rows, tile), 0), 2 * room) < room
    gate = [nn(own_x, go_ref[e]) + nn(oth_x, gx_ref[e]) for e in range(2)]
    out_ref[:, :tile] = jnp.where(first, gate[0], gate[1]).astype(BF)
    up = [nn(own_x, uo_ref[e]) + nn(oth_x, ux_ref[e]) for e in range(2)]
    out_ref[:, tile : 2 * tile] = jnp.where(first, up[0], up[1]).astype(BF)
    back = [nt(own_g, do_ref[e]) + nt(oth_g, dx_ref[e]) for e in range(2)]
    out_ref[:, 2 * tile :] = jnp.where(first, back[0], back[1]).astype(BF)


def activate_kernel(tile, in_ref, out_ref):
    for j in range(in_ref.shape[1] // (3 * tile)):
        at = 3 * tile * j
        gate = in_ref[:, at : at + tile].astype(F32)
        up = in_ref[:, at + tile : at + 2 * tile].astype(F32)
        back = in_ref[:, at + 2 * tile : at + 3 * tile].astype(F32)
        s = jax.nn.sigmoid(gate)
        swish = gate * s
        out_ref[:, at : at + tile] = (swish * up).astype(BF)
        out_ref[:, at + tile : at + 2 * tile] = (back * up * s * (1.0 + gate * (1.0 - s))).astype(BF)
        out_ref[:, at + 2 * tile : at + 3 * tile] = (back * swish).astype(BF)


def contract_kernel(room, tile, act_ref, gate_ref, up_ref, down_ref, out_ref):
    rows = act_ref.shape[0]
    width = gate_ref.shape[1]
    first = lax.rem(lax.broadcasted_iota(jnp.int32, (rows, width), 0), 2 * room) < room
    outs, ins = [], []
    for e in range(2):
        out, inp = jnp.zeros((rows, width), F32), jnp.zeros((rows, width), F32)
        for j in range(gate_ref.shape[2] // tile):
            at, f = 3 * tile * j, tile * j
            out = out + nn(act_ref[:, at : at + tile], down_ref[e, f : f + tile, :])
            inp = inp + nt(act_ref[:, at + tile : at + 2 * tile], gate_ref[e, :, f : f + tile])
            inp = inp + nt(act_ref[:, at + 2 * tile : at + 3 * tile], up_ref[e, :, f : f + tile])
        outs.append(out)
        ins.append(inp)
    out_ref[:, :width] = jnp.where(first, outs[0], outs[1]).astype(BF)
    out_ref[:, width:] = jnp.where(first, ins[0], ins[1]).astype(BF)


def local(
    hidden_in,
    out_grad,
    routes,
    router_weight,
    expert_bias,
    gate_weight,
    up_weight,
    down_weight,
    lengths,
    advantages,
    plan,
):
    fast = ("z", "x")
    columns = lax.axis_size(fast)
    ring, cores = lax.axis_size("y"), lax.axis_size("c")
    core = lax.axis_index("c")
    width = hidden_in.shape[2]
    hidden_units = gate_weight.shape[2]
    experts = router_weight.shape[1]
    tokens, tops = hidden_in.shape[1], routes.shape[2]
    room = tokens * tops // experts + 2
    block = 2 * room
    total = experts * room
    tile = 256
    steps = hidden_units // tile
    x, g = hidden_in[0], out_grad[0]
    routes_t = routes[0].T
    params = pltpu.CompilerParams(vmem_limit_bytes=48 * 2**20)

    smem = pl.BlockSpec(memory_space=pltpu.SMEM)
    vmem = pl.BlockSpec(memory_space=pltpu.VMEM)
    buffer = pl.pallas_call(
        lambda *refs: dispatch_kernel(room, *refs),
        out_shape=jax.ShapeDtypeStruct((total, 2 * width), BF),
        in_specs=[vmem, smem, smem, vmem, vmem],
        out_specs=vmem,
        compiler_params=params,
        name="dispatch",
    )(routes_t, lengths, plan, x, g)

    arrived = lax.all_to_all(
        buffer.reshape(columns, block, 2 * width), fast, split_axis=0, concat_axis=0, tiled=True
    )

    buffer, gate_s, up_s, down_s = lax.optimization_barrier((buffer, gate_weight, up_weight, down_weight))
    swap = [(0, 1), (1, 0)]
    gate_o = lax.ppermute(gate_s, "c", swap)
    up_o = lax.ppermute(up_s, "c", swap)
    down_o = lax.ppermute(down_s, "c", swap)

    share = columns // (ring * cores) * block
    halves = arrived.reshape(ring, cores, share, 2 * width)
    mine = lax.dynamic_index_in_dim(halves, core, 1, keepdims=False).reshape(ring * share, 2 * width)
    yours = lax.dynamic_index_in_dim(halves, 1 - core, 1, keepdims=False).reshape(ring * share, 2 * width)
    other = lax.ppermute(yours, "c", swap)

    half = ring * share
    row_spec = pl.BlockSpec((half, 2 * width), lambda j: (0, 0))
    gate_spec = pl.BlockSpec((2, width, tile), lambda j: (0, 0, j))
    down_spec = pl.BlockSpec((2, tile, width), lambda j: (0, j, 0))
    part = pl.pallas_call(
        lambda *refs: expand_kernel(room, *refs),
        out_shape=jax.ShapeDtypeStruct((half, 3 * hidden_units), BF),
        grid=(steps,),
        in_specs=[row_spec, row_spec, gate_spec, gate_spec, gate_spec, gate_spec, down_spec, down_spec],
        out_specs=pl.BlockSpec((half, 3 * tile), lambda j: (0, j)),
        compiler_params=params,
        name="expand",
    )(mine, other, gate_weight, gate_o, up_weight, up_o, down_weight, down_o)

    logit_part = lax.dot_general(
        router_weight, x, (((0,), (1,)), ((), ())), preferred_element_type=F32
    ).astype(BF)
    part, logit_part = lax.optimization_barrier((part, logit_part))
    summed = lax.psum_scatter(part, "y", scatter_dimension=0, tiled=True)
    logits = jnp.sum(lax.all_gather(logit_part, ("y", "c"), axis=0).astype(F32), axis=0)

    acts = pl.pallas_call(
        lambda *refs: activate_kernel(tile, *refs),
        out_shape=jax.ShapeDtypeStruct((share, 3 * hidden_units), BF),
        in_specs=[vmem],
        out_specs=vmem,
        compiler_params=params,
        name="activate",
    )(summed)
    every = lax.all_gather(acts, ("y", "c"), axis=0, tiled=True)

    pieces = 4
    whole = lambda shape: pl.BlockSpec(shape, lambda i: (0, 0, 0))
    results = pl.pallas_call(
        lambda *refs: contract_kernel(room, tile, *refs),
        out_shape=jax.ShapeDtypeStruct((total, 2 * width), BF),
        grid=(pieces,),
        in_specs=[
            pl.BlockSpec((total // pieces, 3 * hidden_units), lambda i: (i, 0)),
            whole((2, width, hidden_units)),
            whole((2, width, hidden_units)),
            whole((2, hidden_units, width)),
        ],
        out_specs=pl.BlockSpec((total // pieces, 2 * width), lambda i: (i, 0)),
        compiler_params=params,
        name="contract",
    )(every, gate_weight, up_weight, down_weight)
    back = lax.all_to_all(
        results.reshape(columns, block, 2 * width), fast, split_axis=0, concat_axis=0, tiled=True
    ).reshape(total, 2 * width)

    hot, value = ranks(routes_t, experts)
    scores = jax.nn.sigmoid(logits) * hot.astype(F32)
    mixing = (scores / jnp.sum(scores, axis=0, keepdims=True)).astype(BF)
    spread = (jnp.arange(total)[None, :] // room == jnp.arange(experts)[:, None]).astype(BF)
    tn = lambda a, b: lax.dot_general(a, b, (((0,), (0,)), ((), ())), preferred_element_type=F32)
    landing = tn(value, spread) == (jnp.arange(total) % room).astype(F32)[None, :]
    weighting = jnp.where(landing, tn(mixing, spread), 0.0).astype(BF)

    counts = jnp.sum(arrived[:, room - 1, : width // 2 + LEARN_GROUPS].astype(F32), axis=0)
    loads, groups = counts[:experts], counts[width // 2 :]
    ends = jnp.cumsum(lengths[0])
    token_resp = jnp.sum((jnp.arange(tokens)[:, None] >= ends[None, :]).astype(jnp.int32), axis=1)
    resp_hot = token_resp[:, None] == jnp.arange(lengths.shape[1])[None, :]
    token_adv = jnp.sum(jnp.where(resp_hot, advantages[0][None, :], 0.0), axis=1)
    token_plan = jnp.sum(jnp.where(resp_hot, plan[0][None, :], 0), axis=1)
    token_group = token_plan[:, None] == jnp.arange(LEARN_GROUPS)[None, :]
    denominator = jnp.sum(jnp.where(token_group, groups[None, :], 0.0), axis=1)
    token_total = columns * tokens
    token_scale = token_adv * (token_total / LEARN_GROUPS) / denominator
    new_bias = expert_bias + bias_rate * (1.0 - loads / (token_total * tops / experts))

    combined = nn(weighting, back)
    layer_out = combined[:, :width].astype(BF)
    input_grad = (token_scale[:, None] * combined[:, width:]).astype(BF)
    return layer_out[None], input_grad[None], new_bias


def solution(mesh):
    grid = Mesh(mesh.devices.reshape(mesh.shape["dp"] // 2, 2, mesh.shape["expert"] // 4, 4), ("y", "c", "z", "x"))
    dp, expert = ("y", "c"), ("z", "x")
    in_specs = (
        P(expert, None, dp),
        P(expert, None, dp),
        P(expert, None, None),
        P(dp, None),
        P(),
        P(expert, dp, None),
        P(expert, dp, None),
        P(expert, None, dp),
        P(expert, None),
        P(expert, None),
        P(expert, None),
    )
    out_specs = (P(expert, None, dp), P(expert, None, dp), P())
    return jax.shard_map(local, mesh=grid, in_specs=in_specs, out_specs=out_specs, check_vma=False)
```

```python
import jax
import jax.numpy as jnp
import numpy as np
from jax import lax
from jax.experimental import pallas as pl
from jax.experimental.pallas import tpu as pltpu
from jax.sharding import Mesh, PartitionSpec as P

LEARN_GROUPS = 12
bias_rate = 0.1
BF = jnp.bfloat16
F32 = jnp.float32
ROOM_A = 4


def nn(a, b):
    return lax.dot_general(a, b, (((1,), (0,)), ((), ())), preferred_element_type=F32)


def nt(a, b):
    return lax.dot_general(a, b, (((1,), (1,)), ((), ())), preferred_element_type=F32)


def ranks(routes_t, experts):
    tops, rows = routes_t.shape
    ids = lax.broadcasted_iota(jnp.int32, (experts, rows), 0)
    member = ids == routes_t[0:1, :]
    for k in range(1, tops):
        member = member | (ids == routes_t[k : k + 1, :])
    hot = member.astype(F32).astype(BF)
    earlier = (
        lax.broadcasted_iota(jnp.int32, (rows, rows), 0) < lax.broadcasted_iota(jnp.int32, (rows, rows), 1)
    ).astype(F32).astype(BF)
    place = nn(hot, earlier)
    return hot, jnp.where(member, place, -1.0).astype(BF)


def dispatch_kernel(start, room, carry, routes_ref, lens_ref, plan_ref, x_ref, g_ref, *rest):
    buf_ref = rest[-1] if carry else rest[-2]
    total = buf_ref.shape[0]
    experts = total // room
    rows, width = x_ref.shape
    hot, value = ranks(routes_ref[...], experts)
    row = lax.broadcasted_iota(jnp.int32, (total, experts), 0)
    first = lax.broadcasted_iota(jnp.int32, (total, experts), 1) * room
    spread = ((row >= first) & (row < first + room)).astype(F32).astype(BF)
    wide = nn(spread, value)
    line = lax.broadcasted_iota(jnp.int32, (total, rows), 0)
    select = (wide.astype(jnp.int32) == start + lax.rem(line, room)).astype(F32).astype(BF)
    sent = nn(select, x_ref[...])
    if carry:
        loads = nt(jnp.ones((8, rows), BF), hot)[0:1, :]
        group = lax.broadcasted_iota(jnp.int32, (1, width // 2), 1)
        chosen = jnp.zeros((1, width // 2), F32)
        for r in range(plan_ref.shape[1]):
            chosen = chosen + jnp.where(group == plan_ref[:, r : r + 1], lens_ref[:, r : r + 1], 0).astype(F32)
        pad = jnp.zeros((1, width // 2 - experts), F32)
        counts = jnp.concatenate([loads, pad, chosen], axis=1)
        carrier = lax.rem(lax.broadcasted_iota(jnp.int32, (total, width), 0), 2 * room) == room - 1
        sent = jnp.where(carrier, jnp.broadcast_to(counts, sent.shape), sent)
    else:
        router_ref, logit_ref = rest[0], rest[-1]
        logit_ref[...] = nt(router_ref[...], x_ref[...]).astype(BF)
    buf_ref[:, :width] = sent.astype(BF)
    buf_ref[:, width:] = nn(select, g_ref[...]).astype(BF)


def expand_kernel(room, own_ref, oth_ref, go_ref, gx_ref, uo_ref, ux_ref, do_ref, dx_ref, *rest):
    out_ref = rest[-1]
    rows = own_ref.shape[0]
    width = own_ref.shape[1] // 2
    tile = go_ref.shape[2]
    own_x, own_g = own_ref[:, :width], own_ref[:, width:]
    oth_x, oth_g = oth_ref[:, :width], oth_ref[:, width:]
    first = lax.rem(lax.broadcasted_iota(jnp.int32, (rows, tile), 0), 2 * room) < room
    gate = [nn(own_x, go_ref[e]) + nn(oth_x, gx_ref[e]) for e in range(2)]
    out_ref[:, :tile] = jnp.where(first, gate[0], gate[1]).astype(BF)
    up = [nn(own_x, uo_ref[e]) + nn(oth_x, ux_ref[e]) for e in range(2)]
    out_ref[:, tile : 2 * tile] = jnp.where(first, up[0], up[1]).astype(BF)
    back = [nt(own_g, do_ref[e]) + nt(oth_g, dx_ref[e]) for e in range(2)]
    out_ref[:, 2 * tile :] = jnp.where(first, back[0], back[1]).astype(BF)


def activate(gate, up, back):
    s = jax.nn.sigmoid(gate)
    swish = gate * s
    return swish * up, back * up * s * (1.0 + gate * (1.0 - s)), back * swish


def activate_kernel(tile, in_ref, after_ref, out_ref):
    for at in range(0, in_ref.shape[1], 3 * tile):
        parts = [in_ref[:, at + tile * i : at + tile * (i + 1)].astype(F32) for i in range(3)]
        for i, value in enumerate(activate(*parts)):
            out_ref[:, at + tile * i : at + tile * (i + 1)] = value.astype(BF)


def sum_activate_kernel(tile, in_ref, after_ref, out_ref):
    members = in_ref.shape[0]
    for at in range(0, in_ref.shape[2], 3 * tile):
        parts = []
        for i in range(3):
            lanes = slice(at + tile * i, at + tile * (i + 1))
            part = in_ref[0, :, lanes].astype(F32)
            for m in range(1, members):
                part = part + in_ref[m, :, lanes].astype(F32)
            parts.append(part)
        for i, value in enumerate(activate(*parts)):
            for m in range(members):
                out_ref[m, :, at + tile * i : at + tile * (i + 1)] = value.astype(BF)


def contract_kernel(room, tile, act_ref, gate_ref, up_ref, down_ref, *rest):
    out_ref = rest[-1]
    rows = act_ref.shape[0]
    width = gate_ref.shape[1]
    first = lax.rem(lax.broadcasted_iota(jnp.int32, (rows, width), 0), 2 * room) < room
    outs, ins = [], []
    for e in range(2):
        out, inp = jnp.zeros((rows, width), F32), jnp.zeros((rows, width), F32)
        for j in range(gate_ref.shape[2] // tile):
            at, f = 3 * tile * j, tile * j
            out = out + nn(act_ref[:, at : at + tile], down_ref[e, f : f + tile, :])
            inp = inp + nt(act_ref[:, at + tile : at + 2 * tile], gate_ref[e, :, f : f + tile])
            inp = inp + nt(act_ref[:, at + 2 * tile : at + 3 * tile], up_ref[e, :, f : f + tile])
        outs.append(out)
        ins.append(inp)
    out_ref[:, :width] = jnp.where(first, outs[0], outs[1]).astype(BF)
    out_ref[:, width:] = jnp.where(first, ins[0], ins[1]).astype(BF)


def full(v):
    return pl.BlockSpec(v.shape, lambda i: (0,) * len(v.shape))


TILE = 256
FAST = ("z", "x")


def grant(mib):
    return pltpu.CompilerParams(vmem_limit_bytes=mib * 2**20)


def cost(flops, moved):
    return pl.CostEstimate(flops=flops, bytes_accessed=moved, transcendentals=0)


AFTER = pl.BlockSpec(memory_space=pl.ANY)


def dispatch(start, room, carry, routes_t, lengths, plan, x, g, experts, *rest):
    tokens, width = x.shape
    shapes = [jax.ShapeDtypeStruct((experts * room, 2 * width), BF)]
    if not carry:
        shapes.append(jax.ShapeDtypeStruct((experts, tokens), BF))
    outs = pl.pallas_call(
        lambda *refs: dispatch_kernel(start, room, carry, *refs),
        out_shape=shapes,
        grid=(1,),
        in_specs=[full(v) for v in (routes_t, lengths, plan, x, g)] + [full(v) for v in rest[:1]] + [AFTER] * len(rest[1:]),
        out_specs=[full(v) for v in shapes],
        compiler_params=grant(12),
        cost_estimate=cost(2**30, 2**22),
        name="dispatch",
    )(routes_t, lengths, plan, x, g, *rest)
    return outs[0] if carry else outs


def expand(room, mine, other, weights, *after):
    half, wide = mine.shape
    width, hidden_units = weights[0].shape[1:]
    row_spec = pl.BlockSpec((half, wide), lambda j: (0, 0))
    gate_spec = pl.BlockSpec((2, width, TILE), lambda j: (0, 0, j))
    down_spec = pl.BlockSpec((2, TILE, width), lambda j: (0, j, 0))
    return pl.pallas_call(
        lambda *refs: expand_kernel(room, *refs),
        out_shape=jax.ShapeDtypeStruct((half, 3 * hidden_units), BF),
        grid=(hidden_units // TILE,),
        in_specs=[row_spec] * 2 + [gate_spec] * 4 + [down_spec] * 2 + [AFTER] * len(after),
        out_specs=pl.BlockSpec((half, 3 * TILE), lambda j: (0, j)),
        compiler_params=grant(20),
        cost_estimate=cost(2**31, 2**23),
        name="expand",
    )(mine, other, *weights, *after)


def contract(room, pieces, acts, gate, up, down, *after, mib=20):
    total, wide = acts.shape
    width = gate.shape[1]
    whole = lambda w: pl.BlockSpec(w.shape, lambda i: (0, 0, 0))
    return pl.pallas_call(
        lambda *refs: contract_kernel(room, TILE, *refs),
        out_shape=jax.ShapeDtypeStruct((total, 2 * width), BF),
        grid=(pieces,),
        in_specs=[pl.BlockSpec((total // pieces, wide), lambda i: (i, 0)), whole(gate), whole(up), whole(down)]
        + [AFTER] * len(after),
        out_specs=pl.BlockSpec((total // pieces, 2 * width), lambda i: (i, 0)),
        compiler_params=grant(mib),
        cost_estimate=cost(2**31, 2**23),
        name="contract",
    )(acts, gate, up, down, *after)


def local(
    hidden_in,
    out_grad,
    routes,
    router_weight,
    expert_bias,
    gate_weight,
    up_weight,
    down_weight,
    lengths,
    advantages,
    plan,
):
    columns = lax.axis_size(FAST)
    ring, cores = lax.axis_size("y"), lax.axis_size("c")
    core = lax.axis_index("c")
    width = hidden_in.shape[2]
    hidden_units = gate_weight.shape[2]
    experts = router_weight.shape[1]
    tokens, tops = hidden_in.shape[1], routes.shape[2]
    capacity = tokens * tops // experts + 1
    room_a = ROOM_A
    room_b = capacity + 1 - room_a
    x, g = hidden_in[0], out_grad[0]
    routes_t = routes[0].T
    swap = [(0, 1), (1, 0)]

    def exchange(buffer):
        blocks = buffer.reshape(columns, -1, 2 * width)
        return lax.all_to_all(blocks, FAST, split_axis=0, concat_axis=0, tiled=True)

    def halve(arrived):
        share = columns // (ring * cores) * arrived.shape[1]
        halves = arrived.reshape(ring, cores, share, 2 * width)
        pick = lambda c: lax.dynamic_index_in_dim(halves, c, 1, keepdims=False).reshape(ring * share, 2 * width)
        return pick(core), lax.ppermute(pick(1 - core), "c", swap)

    common = (routes_t, lengths, plan, x, g, experts)
    arrived_b = exchange(dispatch(room_a, room_b, True, *common))
    gate_o = lax.ppermute(gate_weight, "c", swap)
    up_o = lax.ppermute(up_weight, "c", swap)
    down_o = lax.ppermute(down_weight, "c", swap)
    weights = (gate_weight, gate_o, up_weight, up_o, down_weight, down_o)

    part_b = expand(room_b, *halve(arrived_b), weights)
    summed_b = lax.psum_scatter(part_b, "y", scatter_dimension=0, tiled=True)

    buffer_a, logit_part = dispatch(0, room_a, False, *common, router_weight.T, part_b)
    arrived_a = exchange(buffer_a)
    part_a = expand(room_a, *halve(arrived_a), weights)
    share_a = part_a.shape[0] // ring
    parts_a = lax.all_to_all(
        part_a.reshape(ring, share_a, 3 * hidden_units), "y", split_axis=0, concat_axis=0, tiled=True
    )

    def act(kernel, summed, after):
        return pl.pallas_call(
            lambda *refs: kernel(TILE, *refs),
            out_shape=jax.ShapeDtypeStruct(summed.shape, BF),
            grid=(1,),
            in_specs=[full(summed), AFTER],
            out_specs=full(summed),
            compiler_params=grant(12),
            cost_estimate=cost(2**26, 2**22),
            name="activate",
        )(summed, after)

    acts_b = act(activate_kernel, summed_b, part_a)
    every_b = lax.all_gather(acts_b, ("y", "c"), axis=0, tiled=True)
    acts_a = act(sum_activate_kernel, parts_a, acts_b)
    every_a = lax.all_to_all(acts_a, "y", split_axis=0, concat_axis=0, tiled=True)
    logits = jnp.sum(lax.all_gather(logit_part, ("y", "c"), axis=0).astype(F32), axis=0)

    every_a = every_a.reshape(ring * share_a, 3 * hidden_units)
    there_a = lax.ppermute(contract(room_a, 1, every_a, gate_o, up_o, down_o), "c", swap)
    here_a = contract(room_a, 1, every_a, gate_weight, up_weight, down_weight)
    here_a, there_a = (v.reshape(ring, 1, share_a, 2 * width) for v in (here_a, there_a))
    which = lax.broadcasted_iota(jnp.int32, (ring, cores, share_a, 2 * width), 1)
    results_a = jnp.where(which == core, here_a, there_a).reshape(columns, 2 * room_a, 2 * width)
    results_b = contract(room_b, 2, every_b, gate_weight, up_weight, down_weight, mib=48)
    results_b = results_b.reshape(columns, 2 * room_b, 2 * width)
    back = exchange(jnp.concatenate([results_a, results_b], axis=1))

    hot, value = ranks(routes_t, experts)
    scores = jax.nn.sigmoid(logits) * hot.astype(F32)
    mixing = (scores / jnp.sum(scores, axis=0, keepdims=True)).astype(BF)
    tn = lambda a, b: lax.dot_general(a, b, (((0,), (0,)), ((), ())), preferred_element_type=F32)

    total = experts * (room_a + room_b)
    block = total // columns
    row = jnp.arange(total)
    line = row % block
    late = line >= 2 * room_a
    line = jnp.where(late, line - 2 * room_a, line)
    room = jnp.where(late, room_b, room_a)
    second = line >= room
    owner = row // block * 2 + second
    slot = line - jnp.where(second, room, 0) + jnp.where(late, room_a, 0)
    spread = (owner[None, :] == jnp.arange(experts)[:, None]).astype(BF)
    landing = tn(value, spread) == slot.astype(F32)[None, :]
    weighting = jnp.where(landing, tn(mixing, spread), 0.0).astype(BF)

    counts = jnp.sum(arrived_b[:, room_b - 1, : width // 2 + LEARN_GROUPS].astype(F32), axis=0)
    loads, groups = counts[:experts], counts[width // 2 :]
    ends = jnp.cumsum(lengths[0])
    token_resp = jnp.sum((jnp.arange(tokens)[:, None] >= ends[None, :]).astype(jnp.int32), axis=1)
    resp_hot = token_resp[:, None] == jnp.arange(lengths.shape[1])[None, :]
    token_adv = jnp.sum(jnp.where(resp_hot, advantages[0][None, :], 0.0), axis=1)
    token_plan = jnp.sum(jnp.where(resp_hot, plan[0][None, :], 0), axis=1)
    token_group = token_plan[:, None] == jnp.arange(LEARN_GROUPS)[None, :]
    denominator = jnp.sum(jnp.where(token_group, groups[None, :], 0.0), axis=1)
    token_total = columns * tokens
    token_scale = token_adv * (token_total / LEARN_GROUPS) / denominator
    new_bias = expert_bias + bias_rate * (1.0 - loads / (token_total * tops / experts))

    combined = nn(weighting, back.reshape(total, 2 * width))
    layer_out = combined[:, :width].astype(BF)
    input_grad = (token_scale[:, None] * combined[:, width:]).astype(BF)
    return layer_out[None], input_grad[None], new_bias


def solution(mesh):
    grid = Mesh(mesh.devices.reshape(mesh.shape["dp"] // 2, 2, mesh.shape["expert"] // 4, 4), ("y", "c", "z", "x"))
    dp, expert = ("y", "c"), ("z", "x")
    in_specs = (
        P(expert, None, dp),
        P(expert, None, dp),
        P(expert, None, None),
        P(dp, None),
        P(),
        P(expert, dp, None),
        P(expert, dp, None),
        P(expert, None, dp),
        P(expert, None),
        P(expert, None),
        P(expert, None),
    )
    out_specs = (P(expert, None, dp), P(expert, None, dp), P())
    return jax.shard_map(local, mesh=grid, in_specs=in_specs, out_specs=out_specs, check_vma=False)
```

```python
import jax
import jax.numpy as jnp
import numpy as np
from jax import lax
from jax.experimental import pallas as pl
from jax.experimental.pallas import tpu as pltpu
from jax.sharding import Mesh, PartitionSpec as P

LEARN_GROUPS = 12
bias_rate = 0.1
BF = jnp.bfloat16
F32 = jnp.float32
PIECES = 3


def nn(a, b):
    return lax.dot_general(a, b, (((1,), (0,)), ((), ())), preferred_element_type=F32)


def nt(a, b):
    return lax.dot_general(a, b, (((1,), (1,)), ((), ())), preferred_element_type=F32)


def ranks(routes_t, experts):
    tops, rows = routes_t.shape
    ids = lax.broadcasted_iota(jnp.int32, (experts, rows), 0)
    member = ids == routes_t[0:1, :]
    for k in range(1, tops):
        member = member | (ids == routes_t[k : k + 1, :])
    hot = member.astype(F32).astype(BF)
    earlier = (
        lax.broadcasted_iota(jnp.int32, (rows, rows), 0) < lax.broadcasted_iota(jnp.int32, (rows, rows), 1)
    ).astype(F32).astype(BF)
    place = nn(hot, earlier)
    return hot, jnp.where(member, place, -1.0).astype(BF)


def dispatch_kernel(room, routes_ref, lens_ref, plan_ref, x_ref, g_ref, buf_ref):
    total = buf_ref.shape[0]
    experts = total // room
    rows, width = x_ref.shape
    hot, value = ranks(routes_ref[...], experts)
    row = lax.broadcasted_iota(jnp.int32, (total, experts), 0)
    first = lax.broadcasted_iota(jnp.int32, (total, experts), 1) * room
    spread = ((row >= first) & (row < first + room)).astype(F32).astype(BF)
    wide = nn(spread, value)
    line = lax.broadcasted_iota(jnp.int32, (total, rows), 0)
    select = (wide.astype(jnp.int32) == lax.rem(line, room)).astype(F32).astype(BF)
    loads = nt(jnp.ones((8, rows), BF), hot)[0:1, :]
    group = lax.broadcasted_iota(jnp.int32, (1, width // 2), 1)
    chosen = jnp.zeros((1, width // 2), F32)
    for r in range(plan_ref.shape[1]):
        chosen = chosen + jnp.where(group == plan_ref[:, r : r + 1], lens_ref[:, r : r + 1], 0).astype(F32)
    pad = jnp.zeros((1, width // 2 - experts), F32)
    counts = jnp.concatenate([loads, pad, chosen], axis=1)
    carrier = lax.rem(lax.broadcasted_iota(jnp.int32, (total, width), 0), 2 * room) == room - 1
    sent = nn(select, x_ref[...])
    buf_ref[:, :width] = jnp.where(carrier, jnp.broadcast_to(counts, sent.shape), sent).astype(BF)
    buf_ref[:, width:] = nn(select, g_ref[...]).astype(BF)


def logits_kernel(router_ref, x_ref, after_ref, out_ref):
    out_ref[...] = nt(router_ref[...], x_ref[...]).astype(BF)


def expand_kernel(room, own_ref, oth_ref, go_ref, gx_ref, uo_ref, ux_ref, do_ref, dx_ref, *rest):
    out_ref = rest[-1]
    rows = own_ref.shape[0]
    width = own_ref.shape[1] // 2
    tile = go_ref.shape[2]
    own_x, own_g = own_ref[:, :width], own_ref[:, width:]
    oth_x, oth_g = oth_ref[:, :width], oth_ref[:, width:]
    first = lax.rem(lax.broadcasted_iota(jnp.int32, (rows, tile), 0), 2 * room) < room
    gate = [nn(own_x, go_ref[e]) + nn(oth_x, gx_ref[e]) for e in range(2)]
    out_ref[:, :tile] = jnp.where(first, gate[0], gate[1]).astype(BF)
    up = [nn(own_x, uo_ref[e]) + nn(oth_x, ux_ref[e]) for e in range(2)]
    out_ref[:, tile : 2 * tile] = jnp.where(first, up[0], up[1]).astype(BF)
    back = [nt(own_g, do_ref[e]) + nt(oth_g, dx_ref[e]) for e in range(2)]
    out_ref[:, 2 * tile :] = jnp.where(first, back[0], back[1]).astype(BF)


def activate(gate, up, back):
    s = jax.nn.sigmoid(gate)
    swish = gate * s
    return swish * up, back * up * s * (1.0 + gate * (1.0 - s)), back * swish


def activate_kernel(tile, in_ref, after_ref, *out_refs):
    for at in range(0, in_ref.shape[1], 3 * tile):
        parts = [in_ref[:, at + tile * i : at + tile * (i + 1)].astype(F32) for i in range(3)]
        for i, value in enumerate(activate(*parts)):
            value = value.reshape(len(out_refs), -1, tile)
            for p, out_ref in enumerate(out_refs):
                out_ref[:, at + tile * i : at + tile * (i + 1)] = value[p].astype(BF)


def combine_kernel(weight_ref, back_ref, scale_ref, out_ref, grad_ref):
    width = out_ref.shape[1]
    out_ref[...] = nn(weight_ref[...], back_ref[:, :width]).astype(BF)
    grad_ref[...] = (scale_ref[...] * nn(weight_ref[...], back_ref[:, width:])).astype(BF)


def contract_kernel(room, tile, pieces, *refs):
    gate_ref, up_ref, down_ref, out_ref = refs[pieces:]
    rows, width = refs[0].shape[0], gate_ref.shape[1]
    first = lax.rem(lax.broadcasted_iota(jnp.int32, (rows, width), 0), 2 * room) < room
    for p in range(pieces):
        act_ref = refs[p]
        outs, ins = [], []
        for e in range(2):
            out, inp = jnp.zeros((rows, width), F32), jnp.zeros((rows, width), F32)
            for j in range(gate_ref.shape[2] // tile):
                at, f = 3 * tile * j, tile * j
                out = out + nn(act_ref[:, at : at + tile], down_ref[e, f : f + tile, :])
                inp = inp + nt(act_ref[:, at + tile : at + 2 * tile], gate_ref[e, :, f : f + tile])
                inp = inp + nt(act_ref[:, at + 2 * tile : at + 3 * tile], up_ref[e, :, f : f + tile])
            outs.append(out)
            ins.append(inp)
        out_ref[p, :, :width] = jnp.where(first, outs[0], outs[1]).astype(BF)
        out_ref[p, :, width:] = jnp.where(first, ins[0], ins[1]).astype(BF)


def full(v):
    return pl.BlockSpec(v.shape, lambda i: (0,) * len(v.shape))


TILE = 256
FAST = ("z", "x")


def grant(mib):
    return pltpu.CompilerParams(vmem_limit_bytes=mib * 2**20)


def cost(flops, moved):
    return pl.CostEstimate(flops=flops, bytes_accessed=moved, transcendentals=0)


AFTER = pl.BlockSpec(memory_space=pl.ANY)


def call(kernel, operands, shapes, name, flops, moved, after=(), mib=12):
    shapes = [jax.ShapeDtypeStruct(shape, dtype) for shape, dtype in shapes]
    outs = pl.pallas_call(
        kernel,
        out_shape=shapes,
        grid=(1,),
        in_specs=[full(v) for v in operands] + [AFTER] * len(after),
        out_specs=[full(v) for v in shapes],
        compiler_params=grant(mib),
        cost_estimate=cost(flops, moved),
        name=name,
    )(*operands, *after)
    return outs if len(outs) > 1 else outs[0]


def expand(room, mine, other, weights, *after):
    half, wide = mine.shape
    width, hidden_units = weights[0].shape[1:]
    row_spec = pl.BlockSpec((half, wide), lambda j: (0, 0))
    gate_spec = pl.BlockSpec((2, width, TILE), lambda j: (0, 0, j))
    down_spec = pl.BlockSpec((2, TILE, width), lambda j: (0, j, 0))
    return pl.pallas_call(
        lambda *refs: expand_kernel(room, *refs),
        out_shape=jax.ShapeDtypeStruct((half, 3 * hidden_units), BF),
        grid=(hidden_units // TILE,),
        in_specs=[row_spec] * 2 + [gate_spec] * 4 + [down_spec] * 2 + [AFTER] * len(after),
        out_specs=pl.BlockSpec((half, 3 * TILE), lambda j: (0, j)),
        compiler_params=grant(20),
        cost_estimate=cost(2**31, 2**23),
        name="expand",
    )(mine, other, *weights, *after)


def local(
    hidden_in,
    out_grad,
    routes,
    router_weight,
    expert_bias,
    gate_weight,
    up_weight,
    down_weight,
    lengths,
    advantages,
    plan,
):
    columns = lax.axis_size(FAST)
    ring, cores = lax.axis_size("y"), lax.axis_size("c")
    core = lax.axis_index("c")
    width = hidden_in.shape[2]
    hidden_units = gate_weight.shape[2]
    experts = router_weight.shape[1]
    tokens, tops = hidden_in.shape[1], routes.shape[2]
    room = tokens * tops // experts + 2
    block, total = 2 * room, experts * room
    x, g = hidden_in[0], out_grad[0]
    routes_t = routes[0].T
    swap = [(0, 1), (1, 0)]

    def exchange(buffer):
        blocks = buffer.reshape(columns, block, 2 * width)
        return lax.all_to_all(blocks, FAST, split_axis=0, concat_axis=0, tiled=True)

    buffer = call(
        lambda *refs: dispatch_kernel(room, *refs),
        (routes_t, lengths, plan, x, g),
        [((total, 2 * width), BF)],
        "dispatch",
        2**30,
        2**21,
        mib=56,
    )
    arrived = exchange(buffer)
    gate_o = lax.ppermute(gate_weight, "c", swap)
    up_o = lax.ppermute(up_weight, "c", swap)
    down_o = lax.ppermute(down_weight, "c", swap)
    weights = (gate_weight, gate_o, up_weight, up_o, down_weight, down_o)

    half = columns // cores * block
    halves = arrived.reshape(columns // (ring * cores), ring, cores, block, 2 * width)
    pick = lambda c: lax.dynamic_index_in_dim(halves, c, 2, keepdims=False).swapaxes(0, 1).reshape(half, 2 * width)
    other = lax.ppermute(pick(1 - core), "c", swap)
    part = expand(room, pick(core), other, weights)
    summed = lax.psum_scatter(part, "y", scatter_dimension=0, tiled=True)

    logit_part = call(
        logits_kernel, (router_weight.T, x), [((experts, tokens), BF)], "logits", 2**23, 2**18, after=(part,)
    )
    logit_parts = lax.all_gather(logit_part, ("y", "c"), axis=0)

    share = half // ring // PIECES
    acts = call(
        lambda *refs: activate_kernel(TILE, *refs),
        (summed,),
        [((share, 3 * hidden_units), BF)] * PIECES,
        "activate",
        2**26,
        2**21,
        after=(logit_parts,),
        mib=56,
    )
    every = [lax.all_gather(v, "y", axis=0, tiled=True) for v in acts]

    def contract(gate, up, down):
        return call(
            lambda *refs: contract_kernel(room, TILE, PIECES, *refs),
            (*every, gate, up, down),
            [((PIECES, ring * share, 2 * width), BF)],
            "contract",
            2**31,
            2**23,
            mib=24,
        ).reshape(PIECES, ring, 1, share, 2 * width)

    there = lax.ppermute(contract(gate_o, up_o, down_o), "c", swap)
    here = contract(gate_weight, up_weight, down_weight)
    which = lax.broadcasted_iota(jnp.int32, (PIECES, ring, cores, share, 2 * width), 2)
    back = exchange(jnp.where(which == core, here, there))
    logits = jnp.sum(logit_parts.astype(F32), axis=0)

    hot, value = ranks(routes_t, experts)
    scores = jax.nn.sigmoid(logits) * hot.astype(F32)
    mixing = (scores / jnp.sum(scores, axis=0, keepdims=True)).astype(BF)
    tn = lambda a, b: lax.dot_general(a, b, (((0,), (0,)), ((), ())), preferred_element_type=F32)

    spread = (jnp.arange(total)[None, :] // room == jnp.arange(experts)[:, None]).astype(BF)
    landing = tn(value, spread) == (jnp.arange(total) % room).astype(F32)[None, :]
    weighting = jnp.where(landing, tn(mixing, spread), 0.0).astype(BF)

    counts = jnp.sum(arrived[:, room - 1, : width // 2 + LEARN_GROUPS].astype(F32), axis=0)
    loads, groups = counts[:experts], counts[width // 2 :]
    ends = jnp.cumsum(lengths[0])
    token_resp = jnp.sum((jnp.arange(tokens)[:, None] >= ends[None, :]).astype(jnp.int32), axis=1)
    resp_hot = token_resp[:, None] == jnp.arange(lengths.shape[1])[None, :]
    token_adv = jnp.sum(jnp.where(resp_hot, advantages[0][None, :], 0.0), axis=1)
    token_plan = jnp.sum(jnp.where(resp_hot, plan[0][None, :], 0), axis=1)
    token_group = token_plan[:, None] == jnp.arange(LEARN_GROUPS)[None, :]
    denominator = jnp.sum(jnp.where(token_group, groups[None, :], 0.0), axis=1)
    token_total = columns * tokens
    token_scale = token_adv * (token_total / LEARN_GROUPS) / denominator
    new_bias = expert_bias + bias_rate * (1.0 - loads / (token_total * tops / experts))

    layer_out, input_grad = call(
        combine_kernel,
        (weighting, back.reshape(total, 2 * width), token_scale[:, None]),
        [((tokens, width), BF)] * 2,
        "combine",
        2**27,
        2**21,
    )
    return layer_out[None], input_grad[None], new_bias


def solution(mesh):
    grid = Mesh(mesh.devices.reshape(mesh.shape["dp"] // 2, 2, mesh.shape["expert"] // 4, 4), ("y", "c", "z", "x"))
    dp, expert = ("y", "c"), ("z", "x")
    in_specs = (
        P(expert, None, dp),
        P(expert, None, dp),
        P(expert, None, None),
        P(dp, None),
        P(),
        P(expert, dp, None),
        P(expert, dp, None),
        P(expert, None, dp),
        P(expert, None),
        P(expert, None),
        P(expert, None),
    )
    out_specs = (P(expert, None, dp), P(expert, None, dp), P())
    return jax.shard_map(local, mesh=grid, in_specs=in_specs, out_specs=out_specs, check_vma=False)
```

```python
import jax
import jax.numpy as jnp
import numpy as np
from jax import lax
from jax.experimental import pallas as pl
from jax.experimental.pallas import tpu as pltpu
from jax.sharding import Mesh, PartitionSpec as P

LEARN_GROUPS = 12
bias_rate = 0.1
BF = jnp.bfloat16
F32 = jnp.float32


def nn(a, b):
    return lax.dot_general(a, b, (((1,), (0,)), ((), ())), preferred_element_type=F32)


def nt(a, b):
    return lax.dot_general(a, b, (((1,), (1,)), ((), ())), preferred_element_type=F32)


def ranks(routes_t, experts):
    tops, rows = routes_t.shape
    ids = lax.broadcasted_iota(jnp.int32, (experts, rows), 0)
    member = ids == routes_t[0:1, :]
    for k in range(1, tops):
        member = member | (ids == routes_t[k : k + 1, :])
    hot = member.astype(F32).astype(BF)
    earlier = (
        lax.broadcasted_iota(jnp.int32, (rows, rows), 0) < lax.broadcasted_iota(jnp.int32, (rows, rows), 1)
    ).astype(F32).astype(BF)
    place = nn(hot, earlier)
    return hot, jnp.where(member, place, -1.0).astype(BF)


def dispatch_kernel(room, routes_ref, lens_ref, plan_ref, x_ref, g_ref, buf_ref):
    total = buf_ref.shape[0]
    experts = total // room
    rows, width = x_ref.shape
    hot, value = ranks(routes_ref[...], experts)
    row = lax.broadcasted_iota(jnp.int32, (total, experts), 0)
    first = lax.broadcasted_iota(jnp.int32, (total, experts), 1) * room
    spread = ((row >= first) & (row < first + room)).astype(F32).astype(BF)
    wide = nn(spread, value)
    line = lax.broadcasted_iota(jnp.int32, (total, rows), 0)
    select = (wide.astype(jnp.int32) == lax.rem(line, room)).astype(F32).astype(BF)
    loads = nt(jnp.ones((8, rows), BF), hot)[0:1, :]
    group = lax.broadcasted_iota(jnp.int32, (1, width // 2), 1)
    chosen = jnp.zeros((1, width // 2), F32)
    for r in range(plan_ref.shape[1]):
        chosen = chosen + jnp.where(group == plan_ref[:, r : r + 1], lens_ref[:, r : r + 1], 0).astype(F32)
    pad = jnp.zeros((1, width // 2 - experts), F32)
    counts = jnp.concatenate([loads, pad, chosen], axis=1)
    carrier = lax.rem(lax.broadcasted_iota(jnp.int32, (total, width), 0), 2 * room) == room - 1
    sent = nn(select, x_ref[...])
    buf_ref[:, :width] = jnp.where(carrier, jnp.broadcast_to(counts, sent.shape), sent).astype(BF)
    buf_ref[:, width:] = nn(select, g_ref[...]).astype(BF)


def logits_kernel(router_ref, x_ref, after_ref, out_ref):
    out_ref[...] = nt(router_ref[...], x_ref[...]).astype(BF)


def expand_kernel(room, rows_ref, gate_ref, up_ref, down_ref, out_ref):
    rows = rows_ref.shape[0]
    width = rows_ref.shape[1] // 2
    tile = gate_ref.shape[2]
    x, g = rows_ref[:, :width], rows_ref[:, width:]
    first = lax.rem(lax.broadcasted_iota(jnp.int32, (rows, tile), 0), 2 * room) < room
    out_ref[:, :tile] = jnp.where(first, nn(x, gate_ref[0]), nn(x, gate_ref[1])).astype(BF)
    out_ref[:, tile : 2 * tile] = jnp.where(first, nn(x, up_ref[0]), nn(x, up_ref[1])).astype(BF)
    out_ref[:, 2 * tile :] = jnp.where(first, nt(g, down_ref[0]), nt(g, down_ref[1])).astype(BF)


def expand_add_kernel(room, rows_ref, gate_ref, up_ref, down_ref, other_ref, out_ref):
    rows = rows_ref.shape[0]
    width = rows_ref.shape[1] // 2
    tile = gate_ref.shape[2]
    x, g = rows_ref[:, :width], rows_ref[:, width:]
    first = lax.rem(lax.broadcasted_iota(jnp.int32, (rows, tile), 0), 2 * room) < room
    parts = (
        jnp.where(first, nn(x, gate_ref[0]), nn(x, gate_ref[1])),
        jnp.where(first, nn(x, up_ref[0]), nn(x, up_ref[1])),
        jnp.where(first, nt(g, down_ref[0]), nt(g, down_ref[1])),
    )
    for i, part in enumerate(parts):
        lanes = slice(tile * i, tile * (i + 1))
        out_ref[:, lanes] = (part + other_ref[:, lanes].astype(F32)).astype(BF)


def home_kernel(
    room, routes_ref, logits_ref, lens_ref, adv_ref, plan_ref, bias_ref, counts_ref, weight_ref, scale_ref, new_ref
):
    tokens, total = weight_ref.shape
    experts = total // room
    hot, value = ranks(routes_ref[...], experts)
    logits = logits_ref[0].astype(F32)
    for m in range(1, logits_ref.shape[0]):
        logits = logits + logits_ref[m].astype(F32)
    scores = jax.nn.sigmoid(logits) * hot.astype(F32)
    mixing = (scores / jnp.sum(scores, axis=0, keepdims=True)).astype(BF)
    row = lax.broadcasted_iota(jnp.int32, (total, experts), 0)
    begin = lax.broadcasted_iota(jnp.int32, (total, experts), 1) * room
    spread = ((row >= begin) & (row < begin + room)).astype(F32).astype(BF)
    line = lax.rem(lax.broadcasted_iota(jnp.int32, (total, tokens), 0), room)
    landing = nn(spread, value).astype(jnp.int32) == line
    weight_ref[...] = jnp.where(landing, nn(spread, mixing), 0.0).T.astype(BF)
    half = counts_ref.shape[1] // 2
    groups = counts_ref[:, half:]
    group = lax.broadcasted_iota(jnp.int32, (1, half), 1)
    token = lax.broadcasted_iota(jnp.int32, (tokens, 1), 0)
    mean = experts // 2 * tokens / LEARN_GROUPS
    start, scale = jnp.zeros((1, 1), jnp.int32), jnp.zeros((tokens, 1), F32)
    for r in range(plan_ref.shape[1]):
        end = start + lens_ref[:, r : r + 1]
        size = jnp.sum(jnp.where(group == plan_ref[:, r : r + 1], groups, 0.0), axis=1, keepdims=True)
        scale = jnp.where((token >= start) & (token < end), adv_ref[:, r : r + 1] * mean / size, scale)
        start = end
    scale_ref[...] = scale
    load = routes_ref.shape[0] * experts // 2 * tokens / experts
    new_ref[...] = bias_ref[...] + bias_rate * (1.0 - counts_ref[:, :experts] / load)


def activate(gate, up, back):
    s = jax.nn.sigmoid(gate)
    swish = gate * s
    return swish * up, back * up * s * (1.0 + gate * (1.0 - s)), back * swish


def activate_kernel(tile, in_ref, after_ref, out_ref):
    for at in range(0, in_ref.shape[1], 3 * tile):
        parts = [in_ref[:, at + tile * i : at + tile * (i + 1)].astype(F32) for i in range(3)]
        for i, value in enumerate(activate(*parts)):
            out_ref[:, at + tile * i : at + tile * (i + 1)] = value.astype(BF)


def combine_kernel(weight_ref, back_ref, scale_ref, out_ref, grad_ref):
    width = out_ref.shape[1]
    out_ref[...] = nn(weight_ref[...], back_ref[:, :width]).astype(BF)
    grad_ref[...] = (scale_ref[...] * nn(weight_ref[...], back_ref[:, width:])).astype(BF)


def contract_kernel(room, tile, act_ref, gate_ref, up_ref, down_ref, after_ref, out_ref):
    rows, width = act_ref.shape[0], gate_ref.shape[1]
    first = lax.rem(lax.broadcasted_iota(jnp.int32, (rows, width), 0), 2 * room) < room
    outs, ins = [], []
    for e in range(2):
        out, inp = jnp.zeros((rows, width), F32), jnp.zeros((rows, width), F32)
        for j in range(gate_ref.shape[2] // tile):
            at, f = 3 * tile * j, tile * j
            out = out + nn(act_ref[:, at : at + tile], down_ref[e, f : f + tile, :])
            inp = inp + nt(act_ref[:, at + tile : at + 2 * tile], gate_ref[e, :, f : f + tile])
            inp = inp + nt(act_ref[:, at + 2 * tile : at + 3 * tile], up_ref[e, :, f : f + tile])
        outs.append(out)
        ins.append(inp)
    out_ref[:, :width] = jnp.where(first, outs[0], outs[1]).astype(BF)
    out_ref[:, width:] = jnp.where(first, ins[0], ins[1]).astype(BF)


def full(v):
    return pl.BlockSpec(v.shape, lambda i: (0,) * len(v.shape))


TILE = 256
FAST = ("z", "x")


def grant(mib):
    return pltpu.CompilerParams(vmem_limit_bytes=mib * 2**20)


def cost(flops, moved):
    return pl.CostEstimate(flops=flops, bytes_accessed=moved, transcendentals=0)


AFTER = pl.BlockSpec(memory_space=pl.ANY)


def call(kernel, operands, shapes, name, flops, moved, after=(), mib=12):
    shapes = [jax.ShapeDtypeStruct(shape, dtype) for shape, dtype in shapes]
    outs = pl.pallas_call(
        kernel,
        out_shape=shapes,
        grid=(1,),
        in_specs=[full(v) for v in operands] + [AFTER] * len(after),
        out_specs=[full(v) for v in shapes],
        compiler_params=grant(mib),
        cost_estimate=cost(flops, moved),
        name=name,
    )(*operands, *after)
    return outs if len(outs) > 1 else outs[0]


def expand(room, rows, weights, *other):
    half, wide = rows.shape
    width, hidden_units = weights[0].shape[1:]
    kernel = expand_add_kernel if other else expand_kernel
    row_spec = pl.BlockSpec((half, wide), lambda j: (0, 0))
    gate_spec = pl.BlockSpec((2, width, TILE), lambda j: (0, 0, j))
    down_spec = pl.BlockSpec((2, TILE, width), lambda j: (0, j, 0))
    out_spec = pl.BlockSpec((half, 3 * TILE), lambda j: (0, j))
    return pl.pallas_call(
        lambda *refs: kernel(room, *refs),
        out_shape=jax.ShapeDtypeStruct((half, 3 * hidden_units), BF),
        grid=(hidden_units // TILE,),
        in_specs=[row_spec, gate_spec, gate_spec, down_spec] + [out_spec] * len(other),
        out_specs=out_spec,
        compiler_params=grant(20),
        cost_estimate=cost(2**31, 2**23),
        name="expand",
    )(rows, *weights, *other)


def contract(room, acts, weights, after, pieces=4):
    total, wide = acts.shape
    width = weights[0].shape[1]
    whole = lambda w: pl.BlockSpec(w.shape, lambda i: (0, 0, 0))
    return pl.pallas_call(
        lambda *refs: contract_kernel(room, TILE, *refs),
        out_shape=jax.ShapeDtypeStruct((total, 2 * width), BF),
        grid=(pieces,),
        in_specs=[pl.BlockSpec((total // pieces, wide), lambda i: (i, 0))] + [whole(w) for w in weights] + [AFTER],
        out_specs=pl.BlockSpec((total // pieces, 2 * width), lambda i: (i, 0)),
        compiler_params=grant(20),
        cost_estimate=cost(2**31, 2**23),
        name="contract",
    )(acts, *weights, after)


def local(
    hidden_in,
    out_grad,
    routes,
    router_weight,
    expert_bias,
    gate_weight,
    up_weight,
    down_weight,
    lengths,
    advantages,
    plan,
):
    columns = lax.axis_size(FAST)
    ring, cores = lax.axis_size("y"), lax.axis_size("c")
    core = lax.axis_index("c")
    width = hidden_in.shape[2]
    hidden_units = gate_weight.shape[2]
    experts = router_weight.shape[1]
    tokens, tops = hidden_in.shape[1], routes.shape[2]
    room = tokens * tops // experts + 2
    block, total = 2 * room, experts * room
    x, g = hidden_in[0], out_grad[0]
    routes_t = routes[0].T
    swap = [(0, 1), (1, 0)]

    def exchange(buffer):
        blocks = buffer.reshape(columns, block, 2 * width)
        return lax.all_to_all(blocks, FAST, split_axis=0, concat_axis=0, tiled=True)

    buffer = call(
        lambda *refs: dispatch_kernel(room, *refs),
        (routes_t, lengths, plan, x, g),
        [((total, 2 * width), BF)],
        "dispatch",
        2**30,
        2**21,
        mib=56,
    )
    arrived = exchange(buffer)
    weights = (gate_weight, up_weight, down_weight)

    half = columns // cores * block
    halves = arrived.reshape(ring, cores, half // ring, 2 * width)
    pick = lambda c: lax.dynamic_index_in_dim(halves, c, 1, keepdims=False).reshape(half, 2 * width)
    other = lax.ppermute(expand(room, pick(1 - core), weights), "c", swap)
    mine = expand(room, pick(core), weights)
    part = mine + other
    summed = lax.psum_scatter(part, "y", scatter_dimension=0, tiled=True)

    logit_part = call(
        logits_kernel, (router_weight.T, x), [((experts, tokens), BF)], "logits", 2**23, 2**18, after=(part,)
    )
    logit_parts = lax.all_gather(logit_part, ("y", "c"), axis=0)
    counts = jnp.sum(arrived[:, room - 1, :width].astype(F32), axis=0, keepdims=True)
    weighting, token_scale, new_bias = call(
        lambda *refs: home_kernel(room, *refs),
        (routes_t, logit_parts, lengths, advantages, plan, expert_bias[None], counts),
        [((tokens, total), BF), ((tokens, 1), F32), ((1, experts), F32)],
        "home",
        2**28,
        2**21,
    )

    acts = call(
        lambda *refs: activate_kernel(TILE, *refs),
        (summed,),
        [(summed.shape, BF)],
        "activate",
        2**26,
        2**20,
        after=(weighting,),
        mib=60,
    )
    every = lax.all_gather(acts, ("y", "c"), axis=0, tiled=True)
    back = exchange(contract(room, every, weights, weighting))
    layer_out, input_grad = call(
        combine_kernel,
        (weighting, back.reshape(total, 2 * width), token_scale),
        [((tokens, width), BF)] * 2,
        "combine",
        2**27,
        2**21,
    )
    new_bias = new_bias[0]
    return layer_out[None], input_grad[None], new_bias


def solution(mesh):
    grid = Mesh(mesh.devices.reshape(mesh.shape["dp"] // 2, 2, mesh.shape["expert"] // 4, 4), ("y", "c", "z", "x"))
    dp, expert = ("y", "c"), ("z", "x")
    in_specs = (
        P(expert, None, dp),
        P(expert, None, dp),
        P(expert, None, None),
        P(dp, None),
        P(),
        P(expert, dp, None),
        P(expert, dp, None),
        P(expert, None, dp),
        P(expert, None),
        P(expert, None),
        P(expert, None),
    )
    out_specs = (P(expert, None, dp), P(expert, None, dp), P())
    return jax.shard_map(local, mesh=grid, in_specs=in_specs, out_specs=out_specs, check_vma=False)
```

```python
import jax
import jax.numpy as jnp
from jax import lax
from jax.experimental import pallas as pl
from jax.experimental.pallas import tpu as pltpu
from jax.sharding import PartitionSpec as P

LEARN_GROUPS = 12
bias_rate = 0.1
BF = jnp.bfloat16
F32 = jnp.float32


def nn(a, b):
    return lax.dot_general(a, b, (((1,), (0,)), ((), ())), preferred_element_type=F32)


def nt(a, b):
    return lax.dot_general(a, b, (((1,), (1,)), ((), ())), preferred_element_type=F32)


def ranks(routes_t, experts):
    tops, rows = routes_t.shape
    ids = lax.broadcasted_iota(jnp.int32, (experts, rows), 0)
    member = ids == routes_t[0:1, :]
    for k in range(1, tops):
        member = member | (ids == routes_t[k : k + 1, :])
    hot = member.astype(F32).astype(BF)
    earlier = (
        lax.broadcasted_iota(jnp.int32, (rows, rows), 0) < lax.broadcasted_iota(jnp.int32, (rows, rows), 1)
    ).astype(F32).astype(BF)
    place = nn(hot, earlier)
    return hot, jnp.where(member, place, -1.0).astype(BF)


def dispatch_kernel(room, routes_ref, lens_ref, plan_ref, x_ref, g_ref, buf_ref):
    total = buf_ref.shape[0]
    experts = total // room
    rows, width = x_ref.shape
    hot, value = ranks(routes_ref[...], experts)
    row = lax.broadcasted_iota(jnp.int32, (total, experts), 0)
    first = lax.broadcasted_iota(jnp.int32, (total, experts), 1) * room
    spread = ((row >= first) & (row < first + room)).astype(F32).astype(BF)
    wide = nn(spread, value)
    line = lax.broadcasted_iota(jnp.int32, (total, rows), 0)
    select = (wide.astype(jnp.int32) == lax.rem(line, room)).astype(F32).astype(BF)
    loads = nt(jnp.ones((8, rows), BF), hot)[0:1, :]
    group = lax.broadcasted_iota(jnp.int32, (1, width // 2), 1)
    chosen = jnp.zeros((1, width // 2), F32)
    for r in range(plan_ref.shape[1]):
        chosen = chosen + jnp.where(group == plan_ref[:, r : r + 1], lens_ref[:, r : r + 1], 0).astype(F32)
    pad = jnp.zeros((1, width // 2 - experts), F32)
    counts = jnp.concatenate([loads, pad, chosen], axis=1)
    carrier = lax.rem(lax.broadcasted_iota(jnp.int32, (total, width), 0), 2 * room) == room - 1
    sent = nn(select, x_ref[...])
    buf_ref[:, :width] = jnp.where(carrier, jnp.broadcast_to(counts, sent.shape), sent).astype(BF)
    buf_ref[:, width:] = nn(select, g_ref[...]).astype(BF)


def logits_kernel(router_ref, x_ref, after_ref, out_ref):
    out_ref[...] = nt(router_ref[...], x_ref[...]).astype(BF)


def expand_kernel(room, own_ref, oth_ref, go_ref, gx_ref, uo_ref, ux_ref, do_ref, dx_ref, out_ref):
    rows = own_ref.shape[0]
    width = own_ref.shape[1] // 2
    tile = go_ref.shape[2]
    own_x, own_g = own_ref[:, :width], own_ref[:, width:]
    oth_x, oth_g = oth_ref[:, :width], oth_ref[:, width:]
    first = lax.rem(lax.broadcasted_iota(jnp.int32, (rows, tile), 0), 2 * room) < room
    gate = [nn(own_x, go_ref[e]) + nn(oth_x, gx_ref[e]) for e in range(2)]
    out_ref[:, :tile] = jnp.where(first, gate[0], gate[1]).astype(BF)
    up = [nn(own_x, uo_ref[e]) + nn(oth_x, ux_ref[e]) for e in range(2)]
    out_ref[:, tile : 2 * tile] = jnp.where(first, up[0], up[1]).astype(BF)
    back = [nt(own_g, do_ref[e]) + nt(oth_g, dx_ref[e]) for e in range(2)]
    out_ref[:, 2 * tile :] = jnp.where(first, back[0], back[1]).astype(BF)


def home_kernel(
    room, routes_ref, logits_ref, lens_ref, adv_ref, plan_ref, bias_ref, counts_ref, weight_ref, scale_ref, new_ref
):
    tokens, total = weight_ref.shape
    experts = total // room
    hot, value = ranks(routes_ref[...], experts)
    logits = logits_ref[0].astype(F32)
    for m in range(1, logits_ref.shape[0]):
        logits = logits + logits_ref[m].astype(F32)
    scores = jax.nn.sigmoid(logits) * hot.astype(F32)
    mixing = (scores / jnp.sum(scores, axis=0, keepdims=True)).astype(BF)
    row = lax.broadcasted_iota(jnp.int32, (total, experts), 0)
    begin = lax.broadcasted_iota(jnp.int32, (total, experts), 1) * room
    spread = ((row >= begin) & (row < begin + room)).astype(F32).astype(BF)
    line = lax.rem(lax.broadcasted_iota(jnp.int32, (total, tokens), 0), room)
    landing = nn(spread, value).astype(jnp.int32) == line
    weight_ref[...] = jnp.where(landing, nn(spread, mixing), 0.0).T.astype(BF)
    half = counts_ref.shape[1] // 2
    groups = counts_ref[:, half:]
    group = lax.broadcasted_iota(jnp.int32, (1, half), 1)
    token = lax.broadcasted_iota(jnp.int32, (tokens, 1), 0)
    mean = experts // 2 * tokens / LEARN_GROUPS
    start, scale = jnp.zeros((1, 1), jnp.int32), jnp.zeros((tokens, 1), F32)
    for r in range(plan_ref.shape[1]):
        end = start + lens_ref[:, r : r + 1]
        size = jnp.sum(jnp.where(group == plan_ref[:, r : r + 1], groups, 0.0), axis=1, keepdims=True)
        scale = jnp.where((token >= start) & (token < end), adv_ref[:, r : r + 1] * mean / size, scale)
        start = end
    scale_ref[...] = scale
    load = routes_ref.shape[0] * experts // 2 * tokens / experts
    new_ref[...] = bias_ref[...] + bias_rate * (1.0 - counts_ref[:, :experts] / load)


def activate(gate, up, back):
    s = jax.nn.sigmoid(gate)
    swish = gate * s
    return swish * up, back * up * s * (1.0 + gate * (1.0 - s)), back * swish


def activate_kernel(tile, in_ref, after_ref, out_ref):
    for at in range(0, in_ref.shape[1], 3 * tile):
        parts = [in_ref[:, at + tile * i : at + tile * (i + 1)].astype(F32) for i in range(3)]
        for i, value in enumerate(activate(*parts)):
            out_ref[:, at + tile * i : at + tile * (i + 1)] = value.astype(BF)


def combine_kernel(weight_ref, back_ref, scale_ref, out_ref, grad_ref):
    width = out_ref.shape[1]
    out_ref[...] = nn(weight_ref[...], back_ref[:, :width]).astype(BF)
    grad_ref[...] = (scale_ref[...] * nn(weight_ref[...], back_ref[:, width:])).astype(BF)


def contract_kernel(room, tile, act_ref, gate_ref, up_ref, down_ref, after_ref, out_ref):
    rows, width = act_ref.shape[0], gate_ref.shape[1]
    first = lax.rem(lax.broadcasted_iota(jnp.int32, (rows, width), 0), 2 * room) < room
    outs, ins = [], []
    for e in range(2):
        out, inp = jnp.zeros((rows, width), F32), jnp.zeros((rows, width), F32)
        for j in range(gate_ref.shape[2] // tile):
            at, f = 3 * tile * j, tile * j
            out = out + nn(act_ref[:, at : at + tile], down_ref[e, f : f + tile, :])
            inp = inp + nt(act_ref[:, at + tile : at + 2 * tile], gate_ref[e, :, f : f + tile])
            inp = inp + nt(act_ref[:, at + 2 * tile : at + 3 * tile], up_ref[e, :, f : f + tile])
        outs.append(out)
        ins.append(inp)
    out_ref[:, :width] = jnp.where(first, outs[0], outs[1]).astype(BF)
    out_ref[:, width:] = jnp.where(first, ins[0], ins[1]).astype(BF)


def full(v):
    return pl.BlockSpec(v.shape, lambda i: (0,) * len(v.shape))


TILE = 256


def grant(mib):
    return pltpu.CompilerParams(vmem_limit_bytes=mib * 2**20)


def cost(flops, moved):
    return pl.CostEstimate(flops=flops, bytes_accessed=moved, transcendentals=0)


AFTER = pl.BlockSpec(memory_space=pl.ANY)


def call(kernel, operands, shapes, name, flops, moved, after=(), mib=12):
    shapes = [jax.ShapeDtypeStruct(shape, dtype) for shape, dtype in shapes]
    outs = pl.pallas_call(
        kernel,
        out_shape=shapes,
        grid=(1,),
        in_specs=[full(v) for v in operands] + [AFTER] * len(after),
        out_specs=[full(v) for v in shapes],
        compiler_params=grant(mib),
        cost_estimate=cost(flops, moved),
        name=name,
    )(*operands, *after)
    return outs if len(outs) > 1 else outs[0]


def expand(room, mine, other, weights):
    half, wide = mine.shape
    width, hidden_units = weights[0].shape[1:]
    row_spec = pl.BlockSpec((half, wide), lambda j: (0, 0))
    gate_spec = pl.BlockSpec((2, width, TILE), lambda j: (0, 0, j))
    down_spec = pl.BlockSpec((2, TILE, width), lambda j: (0, j, 0))
    return pl.pallas_call(
        lambda *refs: expand_kernel(room, *refs),
        out_shape=jax.ShapeDtypeStruct((half, 3 * hidden_units), BF),
        grid=(hidden_units // TILE,),
        in_specs=[row_spec] * 2 + [gate_spec] * 4 + [down_spec] * 2,
        out_specs=pl.BlockSpec((half, 3 * TILE), lambda j: (0, j)),
        compiler_params=grant(20),
        cost_estimate=cost(2**31, 2**23),
        name="expand",
    )(mine, other, *weights)


def contract(room, acts, weights, after, pieces=2):
    total, wide = acts.shape
    width = weights[0].shape[1]
    whole = lambda w: pl.BlockSpec(w.shape, lambda i: (0, 0, 0))
    return pl.pallas_call(
        lambda *refs: contract_kernel(room, TILE, *refs),
        out_shape=jax.ShapeDtypeStruct((total, 2 * width), BF),
        grid=(pieces,),
        in_specs=[pl.BlockSpec((total // pieces, wide), lambda i: (i, 0))] + [whole(w) for w in weights] + [AFTER],
        out_specs=pl.BlockSpec((total // pieces, 2 * width), lambda i: (i, 0)),
        compiler_params=grant(20),
        cost_estimate=cost(2**31, 2**23),
        name="contract",
    )(acts, *weights, after)


def local(
    hidden_in,
    out_grad,
    routes,
    router_weight,
    expert_bias,
    gate_weight,
    up_weight,
    down_weight,
    lengths,
    advantages,
    plan,
):
    columns = lax.axis_size("expert")
    cores = 2
    ring = lax.axis_size("dp") // cores
    core = lax.rem(lax.axis_index("dp"), cores)
    rings = [[cores * y for y in range(ring)], [cores * y + 1 for y in reversed(range(ring))]]
    swap = [(i, i ^ 1) for i in range(cores * ring)]
    width = hidden_in.shape[2]
    hidden_units = gate_weight.shape[2]
    experts = router_weight.shape[1]
    tokens, tops = hidden_in.shape[1], routes.shape[2]
    room = tokens * tops // experts + 2
    block, total = 2 * room, experts * room
    x, g = hidden_in[0], out_grad[0]
    routes_t = routes[0].T

    def exchange(buffer):
        blocks = buffer.reshape(columns, block, 2 * width)
        return lax.all_to_all(blocks, "expert", split_axis=0, concat_axis=0, tiled=True)

    buffer = call(
        lambda *refs: dispatch_kernel(room, *refs),
        (routes_t, lengths, plan, x, g),
        [((total, 2 * width), BF)],
        "dispatch",
        2**30,
        2**21,
        mib=56,
    )
    arrived = exchange(buffer)
    gate_o = lax.ppermute(gate_weight, "dp", swap)
    up_o = lax.ppermute(up_weight, "dp", swap)
    down_o = lax.ppermute(down_weight, "dp", swap)

    half = columns // cores * block
    halves = arrived.reshape(ring, cores, half // ring, 2 * width)
    pick = lambda c: lax.dynamic_index_in_dim(halves, c, 1, keepdims=False).reshape(half, 2 * width)
    other = lax.ppermute(pick(1 - core), "dp", swap)
    part = expand(room, pick(core), other, (gate_weight, gate_o, up_weight, up_o, down_weight, down_o))
    summed = lax.psum_scatter(part, "dp", scatter_dimension=0, axis_index_groups=rings, tiled=True)

    logit_part = call(
        logits_kernel, (router_weight.T, x), [((experts, tokens), BF)], "logits", 2**23, 2**18, after=(part,)
    )
    logit_parts = lax.all_gather(logit_part, "dp", axis=0)
    counts = jnp.sum(arrived[:, room - 1, :width].astype(F32), axis=0, keepdims=True)
    weighting, token_scale, new_bias = call(
        lambda *refs: home_kernel(room, *refs),
        (routes_t, logit_parts, lengths, advantages, plan, expert_bias[None], counts),
        [((tokens, total), BF), ((tokens, 1), F32), ((1, experts), F32)],
        "home",
        2**28,
        2**21,
    )

    acts = call(
        lambda *refs: activate_kernel(TILE, *refs),
        (summed,),
        [(summed.shape, BF)],
        "activate",
        2**26,
        2**20,
        after=(weighting,),
        mib=60,
    )
    every = lax.all_gather(acts, "dp", axis=0, axis_index_groups=rings, tiled=True)

    there = lax.ppermute(contract(room, every, (gate_o, up_o, down_o), weighting), "dp", swap)
    here = contract(room, every, (gate_weight, up_weight, down_weight), weighting)
    here, there = (v.reshape(ring, 1, half // ring, 2 * width) for v in (here, there))
    which = lax.broadcasted_iota(jnp.int32, (ring, cores, half // ring, 2 * width), 1)
    back = exchange(jnp.where(which == core, here, there))
    layer_out, input_grad = call(
        combine_kernel,
        (weighting, back.reshape(total, 2 * width), token_scale),
        [((tokens, width), BF)] * 2,
        "combine",
        2**27,
        2**21,
    )
    new_bias = new_bias[0]
    return layer_out[None], input_grad[None], new_bias


def solution(mesh):
    in_specs = (
        P("expert", None, "dp"),
        P("expert", None, "dp"),
        P("expert", None, None),
        P("dp", None),
        P(),
        P("expert", "dp", None),
        P("expert", "dp", None),
        P("expert", None, "dp"),
        P("expert", None),
        P("expert", None),
        P("expert", None),
    )
    out_specs = (P("expert", None, "dp"), P("expert", None, "dp"), P())
    return jax.shard_map(local, mesh=mesh, in_specs=in_specs, out_specs=out_specs, check_vma=False)
```

```python
import jax
import jax.numpy as jnp
from jax import lax
from jax.experimental import pallas as pl
from jax.experimental.pallas import tpu as pltpu
from jax.sharding import PartitionSpec as P

LEARN_GROUPS = 12
bias_rate = 0.1
BF = jnp.bfloat16
F32 = jnp.float32


def nn(a, b):
    return lax.dot_general(a, b, (((1,), (0,)), ((), ())), preferred_element_type=F32)


def nt(a, b):
    return lax.dot_general(a, b, (((1,), (1,)), ((), ())), preferred_element_type=F32)


def ranks(routes_t, experts):
    tops, rows = routes_t.shape
    ids = lax.broadcasted_iota(jnp.int32, (experts, rows), 0)
    member = ids == routes_t[0:1, :]
    for k in range(1, tops):
        member = member | (ids == routes_t[k : k + 1, :])
    hot = member.astype(F32).astype(BF)
    earlier = (
        lax.broadcasted_iota(jnp.int32, (rows, rows), 0) < lax.broadcasted_iota(jnp.int32, (rows, rows), 1)
    ).astype(F32).astype(BF)
    place = nn(hot, earlier)
    return hot, jnp.where(member, place, -1.0).astype(BF)


def dispatch_kernel(room, routes_ref, lens_ref, plan_ref, x_ref, g_ref, buf_ref):
    total = buf_ref.shape[0]
    experts = total // room
    rows, width = x_ref.shape
    hot, value = ranks(routes_ref[...], experts)
    row = lax.broadcasted_iota(jnp.int32, (total, experts), 0)
    first = lax.broadcasted_iota(jnp.int32, (total, experts), 1) * room
    spread = ((row >= first) & (row < first + room)).astype(F32).astype(BF)
    wide = nn(spread, value)
    line = lax.broadcasted_iota(jnp.int32, (total, rows), 0)
    select = (wide.astype(jnp.int32) == lax.rem(line, room)).astype(F32).astype(BF)
    loads = nt(jnp.ones((8, rows), BF), hot)[0:1, :]
    group = lax.broadcasted_iota(jnp.int32, (1, width // 2), 1)
    chosen = jnp.zeros((1, width // 2), F32)
    for r in range(plan_ref.shape[1]):
        chosen = chosen + jnp.where(group == plan_ref[:, r : r + 1], lens_ref[:, r : r + 1], 0).astype(F32)
    pad = jnp.zeros((1, width // 2 - experts), F32)
    counts = jnp.concatenate([loads, pad, chosen], axis=1)
    carrier = lax.rem(lax.broadcasted_iota(jnp.int32, (total, width), 0), 2 * room) == room - 1
    sent = nn(select, x_ref[...])
    buf_ref[:, :width] = jnp.where(carrier, jnp.broadcast_to(counts, sent.shape), sent).astype(BF)
    buf_ref[:, width:] = nn(select, g_ref[...]).astype(BF)


def logits_kernel(router_ref, x_ref, after_ref, out_ref):
    out_ref[...] = nt(router_ref[...], x_ref[...]).astype(BF)


def expand_kernel(room, own_ref, oth_ref, go_ref, gx_ref, uo_ref, ux_ref, do_ref, dx_ref, out_ref):
    rows = own_ref.shape[0]
    width = own_ref.shape[1] // 2
    tile = go_ref.shape[2]
    own_x, own_g = own_ref[:, :width], own_ref[:, width:]
    oth_x, oth_g = oth_ref[:, :width], oth_ref[:, width:]
    first = lax.rem(lax.broadcasted_iota(jnp.int32, (rows, tile), 0), 2 * room) < room
    gate = [nn(own_x, go_ref[e]) + nn(oth_x, gx_ref[e]) for e in range(2)]
    out_ref[:, :tile] = jnp.where(first, gate[0], gate[1]).astype(BF)
    up = [nn(own_x, uo_ref[e]) + nn(oth_x, ux_ref[e]) for e in range(2)]
    out_ref[:, tile : 2 * tile] = jnp.where(first, up[0], up[1]).astype(BF)
    back = [nt(own_g, do_ref[e]) + nt(oth_g, dx_ref[e]) for e in range(2)]
    out_ref[:, 2 * tile :] = jnp.where(first, back[0], back[1]).astype(BF)


def home_kernel(
    room, routes_ref, logits_ref, lens_ref, adv_ref, plan_ref, bias_ref, counts_ref, weight_ref, scale_ref, new_ref
):
    tokens, total = weight_ref.shape
    experts = total // room
    hot, value = ranks(routes_ref[...], experts)
    logits = logits_ref[0].astype(F32)
    for m in range(1, logits_ref.shape[0]):
        logits = logits + logits_ref[m].astype(F32)
    scores = jax.nn.sigmoid(logits) * hot.astype(F32)
    mixing = (scores / jnp.sum(scores, axis=0, keepdims=True)).astype(BF)
    row = lax.broadcasted_iota(jnp.int32, (total, experts), 0)
    begin = lax.broadcasted_iota(jnp.int32, (total, experts), 1) * room
    spread = ((row >= begin) & (row < begin + room)).astype(F32).astype(BF)
    line = lax.rem(lax.broadcasted_iota(jnp.int32, (total, tokens), 0), room)
    landing = nn(spread, value).astype(jnp.int32) == line
    weight_ref[...] = jnp.where(landing, nn(spread, mixing), 0.0).T.astype(BF)
    half = counts_ref.shape[1] // 2
    groups = counts_ref[:, half:]
    group = lax.broadcasted_iota(jnp.int32, (1, half), 1)
    token = lax.broadcasted_iota(jnp.int32, (tokens, 1), 0)
    mean = experts // 2 * tokens / LEARN_GROUPS
    start, scale = jnp.zeros((1, 1), jnp.int32), jnp.zeros((tokens, 1), F32)
    for r in range(plan_ref.shape[1]):
        end = start + lens_ref[:, r : r + 1]
        size = jnp.sum(jnp.where(group == plan_ref[:, r : r + 1], groups, 0.0), axis=1, keepdims=True)
        scale = jnp.where((token >= start) & (token < end), adv_ref[:, r : r + 1] * mean / size, scale)
        start = end
    scale_ref[...] = scale
    load = routes_ref.shape[0] * experts // 2 * tokens / experts
    new_ref[...] = bias_ref[...] + bias_rate * (1.0 - counts_ref[:, :experts] / load)


def activate(gate, up, back):
    s = jax.nn.sigmoid(gate)
    swish = gate * s
    return swish * up, back * up * s * (1.0 + gate * (1.0 - s)), back * swish


def activate_kernel(tile, in_ref, after_ref, out_ref):
    for at in range(0, in_ref.shape[1], 3 * tile):
        parts = [in_ref[:, at + tile * i : at + tile * (i + 1)].astype(F32) for i in range(3)]
        for i, value in enumerate(activate(*parts)):
            out_ref[:, at + tile * i : at + tile * (i + 1)] = value.astype(BF)


def combine_kernel(weight_ref, back_ref, scale_ref, out_ref, grad_ref):
    width = out_ref.shape[1]
    out_ref[...] = nn(weight_ref[...], back_ref[:, :width]).astype(BF)
    grad_ref[...] = (scale_ref[...] * nn(weight_ref[...], back_ref[:, width:])).astype(BF)


def contract_kernel(room, tile, act_ref, gate_ref, up_ref, down_ref, after_ref, out_ref):
    rows, width = act_ref.shape[0], gate_ref.shape[1]
    first = lax.rem(lax.broadcasted_iota(jnp.int32, (rows, width), 0), 2 * room) < room
    outs, ins = [], []
    for e in range(2):
        out, inp = jnp.zeros((rows, width), F32), jnp.zeros((rows, width), F32)
        for j in range(gate_ref.shape[2] // tile):
            at, f = 3 * tile * j, tile * j
            out = out + nn(act_ref[:, at : at + tile], down_ref[e, f : f + tile, :])
            inp = inp + nt(act_ref[:, at + tile : at + 2 * tile], gate_ref[e, :, f : f + tile])
            inp = inp + nt(act_ref[:, at + 2 * tile : at + 3 * tile], up_ref[e, :, f : f + tile])
        outs.append(out)
        ins.append(inp)
    out_ref[:, :width] = jnp.where(first, outs[0], outs[1]).astype(BF)
    out_ref[:, width:] = jnp.where(first, ins[0], ins[1]).astype(BF)


def full(v):
    return pl.BlockSpec(v.shape, lambda i: (0,) * len(v.shape))


TILE = 256


def grant(mib):
    return pltpu.CompilerParams(vmem_limit_bytes=mib * 2**20)


def cost(flops, moved):
    return pl.CostEstimate(flops=flops, bytes_accessed=moved, transcendentals=0)


AFTER = pl.BlockSpec(memory_space=pl.ANY)


def call(kernel, operands, shapes, name, flops, moved, after=(), mib=12):
    shapes = [jax.ShapeDtypeStruct(shape, dtype) for shape, dtype in shapes]
    outs = pl.pallas_call(
        kernel,
        out_shape=shapes,
        grid=(1,),
        in_specs=[full(v) for v in operands] + [AFTER] * len(after),
        out_specs=[full(v) for v in shapes],
        compiler_params=grant(mib),
        cost_estimate=cost(flops, moved),
        name=name,
    )(*operands, *after)
    return outs if len(outs) > 1 else outs[0]


def expand(room, mine, other, weights):
    half, wide = mine.shape
    width, hidden_units = weights[0].shape[1:]
    row_spec = pl.BlockSpec((half, wide), lambda j: (0, 0))
    gate_spec = pl.BlockSpec((2, width, TILE), lambda j: (0, 0, j))
    down_spec = pl.BlockSpec((2, TILE, width), lambda j: (0, j, 0))
    return pl.pallas_call(
        lambda *refs: expand_kernel(room, *refs),
        out_shape=jax.ShapeDtypeStruct((half, 3 * hidden_units), BF),
        grid=(hidden_units // TILE,),
        in_specs=[row_spec] * 2 + [gate_spec] * 4 + [down_spec] * 2,
        out_specs=pl.BlockSpec((half, 3 * TILE), lambda j: (0, j)),
        compiler_params=grant(20),
        cost_estimate=cost(2**31, 2**23),
        name="expand",
    )(mine, other, *weights)


def contract(room, acts, weights, after, pieces=6):
    total, wide = acts.shape
    width = weights[0].shape[1]
    whole = lambda w: pl.BlockSpec(w.shape, lambda i: (0, 0, 0))
    return pl.pallas_call(
        lambda *refs: contract_kernel(room, TILE, *refs),
        out_shape=jax.ShapeDtypeStruct((total, 2 * width), BF),
        grid=(pieces,),
        in_specs=[pl.BlockSpec((total // pieces, wide), lambda i: (i, 0))] + [whole(w) for w in weights] + [AFTER],
        out_specs=pl.BlockSpec((total // pieces, 2 * width), lambda i: (i, 0)),
        compiler_params=grant(52),
        cost_estimate=cost(2**31, 2**23),
        name="contract",
    )(acts, *weights, after)


def local(
    hidden_in,
    out_grad,
    routes,
    router_weight,
    expert_bias,
    gate_weight,
    up_weight,
    down_weight,
    lengths,
    advantages,
    plan,
):
    columns = lax.axis_size("expert")
    cores = 2
    ring = lax.axis_size("dp") // cores
    core = lax.rem(lax.axis_index("dp"), cores)
    rings = [[cores * y + c for y in range(ring)] for c in range(cores)]
    swap = [(i, i ^ 1) for i in range(cores * ring)]
    width = hidden_in.shape[2]
    hidden_units = gate_weight.shape[2]
    experts = router_weight.shape[1]
    tokens, tops = hidden_in.shape[1], routes.shape[2]
    room = tokens * tops // experts + 2
    block, total = 2 * room, experts * room
    x, g = hidden_in[0], out_grad[0]
    routes_t = routes[0].T

    def exchange(buffer):
        blocks = buffer.reshape(columns, block, 2 * width)
        return lax.all_to_all(blocks, "expert", split_axis=0, concat_axis=0, tiled=True)

    buffer = call(
        lambda *refs: dispatch_kernel(room, *refs),
        (routes_t, lengths, plan, x, g),
        [((total, 2 * width), BF)],
        "dispatch",
        2**30,
        2**21,
        mib=56,
    )
    arrived = exchange(buffer)
    gate_o = lax.ppermute(gate_weight, "dp", swap)
    up_o = lax.ppermute(up_weight, "dp", swap)
    down_o = lax.ppermute(down_weight, "dp", swap)

    half = columns // cores * block
    halves = arrived.reshape(ring, cores, half // ring, 2 * width)
    pick = lambda c: lax.dynamic_index_in_dim(halves, c, 1, keepdims=False).reshape(half, 2 * width)
    other = lax.ppermute(pick(1 - core), "dp", swap)
    part = expand(room, pick(core), other, (gate_weight, gate_o, up_weight, up_o, down_weight, down_o))
    summed = lax.psum_scatter(part, "dp", scatter_dimension=0, axis_index_groups=rings, tiled=True)

    logit_part = call(
        logits_kernel, (router_weight.T, x), [((experts, tokens), BF)], "logits", 2**23, 2**18, after=(part,)
    )
    logit_parts = lax.all_gather(logit_part, "dp", axis=0)
    counts = jnp.sum(arrived[:, room - 1, :width].astype(F32), axis=0, keepdims=True)
    weighting, token_scale, new_bias = call(
        lambda *refs: home_kernel(room, *refs),
        (routes_t, logit_parts, lengths, advantages, plan, expert_bias[None], counts),
        [((tokens, total), BF), ((tokens, 1), F32), ((1, experts), F32)],
        "home",
        2**28,
        2**21,
    )

    acts = call(
        lambda *refs: activate_kernel(TILE, *refs),
        (summed,),
        [(summed.shape, BF)],
        "activate",
        2**26,
        2**20,
        after=(weighting,),
        mib=60,
    )
    every = lax.all_gather(acts, "dp", axis=0, tiled=True)
    back = exchange(contract(room, every, (gate_weight, up_weight, down_weight), weighting))
    layer_out, input_grad = call(
        combine_kernel,
        (weighting, back.reshape(total, 2 * width), token_scale),
        [((tokens, width), BF)] * 2,
        "combine",
        2**27,
        2**21,
    )
    new_bias = new_bias[0]
    return layer_out[None], input_grad[None], new_bias


def solution(mesh):
    in_specs = (
        P("expert", None, "dp"),
        P("expert", None, "dp"),
        P("expert", None, None),
        P("dp", None),
        P(),
        P("expert", "dp", None),
        P("expert", "dp", None),
        P("expert", None, "dp"),
        P("expert", None),
        P("expert", None),
        P("expert", None),
    )
    out_specs = (P("expert", None, "dp"), P("expert", None, "dp"), P())
    return jax.shard_map(local, mesh=mesh, in_specs=in_specs, out_specs=out_specs, check_vma=False)
```

```python
import jax
import jax.numpy as jnp
from jax import lax
from jax.experimental import pallas as pl
from jax.experimental.pallas import tpu as pltpu
from jax.sharding import PartitionSpec as P

LEARN_GROUPS = 12
bias_rate = 0.1
BF = jnp.bfloat16
F32 = jnp.float32


def nn(a, b):
    return lax.dot_general(a, b, (((1,), (0,)), ((), ())), preferred_element_type=F32)


def nt(a, b):
    return lax.dot_general(a, b, (((1,), (1,)), ((), ())), preferred_element_type=F32)


def ranks(routes_t, experts):
    tops, rows = routes_t.shape
    ids = lax.broadcasted_iota(jnp.int32, (experts, rows), 0)
    member = ids == routes_t[0:1, :]
    for k in range(1, tops):
        member = member | (ids == routes_t[k : k + 1, :])
    hot = member.astype(F32).astype(BF)
    earlier = (
        lax.broadcasted_iota(jnp.int32, (rows, rows), 0) < lax.broadcasted_iota(jnp.int32, (rows, rows), 1)
    ).astype(F32).astype(BF)
    place = nn(hot, earlier)
    return hot, jnp.where(member, place, -1.0).astype(BF)


def dispatch_kernel(room, routes_ref, lens_ref, plan_ref, x_ref, g_ref, buf_ref):
    total = buf_ref.shape[0]
    experts = total // room
    rows, width = x_ref.shape
    hot, value = ranks(routes_ref[...], experts)
    row = lax.broadcasted_iota(jnp.int32, (total, experts), 0)
    first = lax.broadcasted_iota(jnp.int32, (total, experts), 1) * room
    spread = ((row >= first) & (row < first + room)).astype(F32).astype(BF)
    wide = nn(spread, value)
    line = lax.broadcasted_iota(jnp.int32, (total, rows), 0)
    select = (wide.astype(jnp.int32) == lax.rem(line, room)).astype(F32).astype(BF)
    loads = nt(jnp.ones((8, rows), BF), hot)[0:1, :]
    group = lax.broadcasted_iota(jnp.int32, (1, width // 2), 1)
    chosen = jnp.zeros((1, width // 2), F32)
    for r in range(plan_ref.shape[1]):
        chosen = chosen + jnp.where(group == plan_ref[:, r : r + 1], lens_ref[:, r : r + 1], 0).astype(F32)
    pad = jnp.zeros((1, width // 2 - experts), F32)
    counts = jnp.concatenate([loads, pad, chosen], axis=1)
    carrier = lax.rem(lax.broadcasted_iota(jnp.int32, (total, width), 0), 2 * room) == room - 1
    sent = nn(select, x_ref[...])
    buf_ref[:, :width] = jnp.where(carrier, jnp.broadcast_to(counts, sent.shape), sent).astype(BF)
    buf_ref[:, width:] = nn(select, g_ref[...]).astype(BF)


def logits_kernel(router_ref, x_ref, after_ref, out_ref):
    out_ref[...] = nt(router_ref[...], x_ref[...]).astype(BF)


def expand_kernel(room, core_ref, own_ref, oth_ref, go_ref, gx_ref, uo_ref, ux_ref, do_ref, dx_ref, out_ref):
    rows = oth_ref.shape[0]
    width = oth_ref.shape[1] // 2
    tile = go_ref.shape[2]
    own_x = own_ref[:, :, :width].reshape(rows, width)
    own_g = own_ref[:, :, width:].reshape(rows, width)
    oth_x, oth_g = oth_ref[:, :width], oth_ref[:, width:]
    first = lax.rem(lax.broadcasted_iota(jnp.int32, (rows, tile), 0), 2 * room) < room
    gate = [nn(own_x, go_ref[e]) + nn(oth_x, gx_ref[e]) for e in range(2)]
    out_ref[:, :tile] = jnp.where(first, gate[0], gate[1]).astype(BF)
    up = [nn(own_x, uo_ref[e]) + nn(oth_x, ux_ref[e]) for e in range(2)]
    out_ref[:, tile : 2 * tile] = jnp.where(first, up[0], up[1]).astype(BF)
    back = [nt(own_g, do_ref[e]) + nt(oth_g, dx_ref[e]) for e in range(2)]
    out_ref[:, 2 * tile :] = jnp.where(first, back[0], back[1]).astype(BF)


def home_kernel(
    room, routes_ref, logits_ref, lens_ref, adv_ref, plan_ref, bias_ref, counts_ref, weight_ref, scale_ref, new_ref
):
    tokens, total = weight_ref.shape
    experts = total // room
    hot, value = ranks(routes_ref[...], experts)
    logits = logits_ref[0].astype(F32)
    for m in range(1, logits_ref.shape[0]):
        logits = logits + logits_ref[m].astype(F32)
    scores = jax.nn.sigmoid(logits) * hot.astype(F32)
    mixing = (scores / jnp.sum(scores, axis=0, keepdims=True)).astype(BF)
    row = lax.broadcasted_iota(jnp.int32, (total, experts), 0)
    begin = lax.broadcasted_iota(jnp.int32, (total, experts), 1) * room
    spread = ((row >= begin) & (row < begin + room)).astype(F32).astype(BF)
    line = lax.rem(lax.broadcasted_iota(jnp.int32, (total, tokens), 0), room)
    landing = nn(spread, value).astype(jnp.int32) == line
    weight_ref[...] = jnp.where(landing, nn(spread, mixing), 0.0).T.astype(BF)
    half = counts_ref.shape[1] // 2
    groups = counts_ref[:, half:]
    group = lax.broadcasted_iota(jnp.int32, (1, half), 1)
    token = lax.broadcasted_iota(jnp.int32, (tokens, 1), 0)
    mean = experts // 2 * tokens / LEARN_GROUPS
    start, scale = jnp.zeros((1, 1), jnp.int32), jnp.zeros((tokens, 1), F32)
    for r in range(plan_ref.shape[1]):
        end = start + lens_ref[:, r : r + 1]
        size = jnp.sum(jnp.where(group == plan_ref[:, r : r + 1], groups, 0.0), axis=1, keepdims=True)
        scale = jnp.where((token >= start) & (token < end), adv_ref[:, r : r + 1] * mean / size, scale)
        start = end
    scale_ref[...] = scale
    load = routes_ref.shape[0] * experts // 2 * tokens / experts
    new_ref[...] = bias_ref[...] + bias_rate * (1.0 - counts_ref[:, :experts] / load)


def activate(gate, up, back):
    s = jax.nn.sigmoid(gate)
    swish = gate * s
    return swish * up, back * up * s * (1.0 + gate * (1.0 - s)), back * swish


def activate_kernel(tile, in_ref, after_ref, out_ref):
    for at in range(0, in_ref.shape[1], 3 * tile):
        parts = [in_ref[:, at + tile * i : at + tile * (i + 1)].astype(F32) for i in range(3)]
        for i, value in enumerate(activate(*parts)):
            out_ref[:, at + tile * i : at + tile * (i + 1)] = value.astype(BF)


def combine_kernel(weight_ref, back_ref, scale_ref, out_ref, grad_ref):
    width = out_ref.shape[1]
    out_ref[...] = nn(weight_ref[...], back_ref[:, :width]).astype(BF)
    grad_ref[...] = (scale_ref[...] * nn(weight_ref[...], back_ref[:, width:])).astype(BF)


def contract_kernel(room, tile, act_ref, gate_ref, up_ref, down_ref, after_ref, out_ref):
    rows, width = act_ref.shape[0], gate_ref.shape[1]
    first = lax.rem(lax.broadcasted_iota(jnp.int32, (rows, width), 0), 2 * room) < room
    outs, ins = [], []
    for e in range(2):
        out, inp = jnp.zeros((rows, width), F32), jnp.zeros((rows, width), F32)
        for j in range(gate_ref.shape[2] // tile):
            at, f = 3 * tile * j, tile * j
            out = out + nn(act_ref[:, at : at + tile], down_ref[e, f : f + tile, :])
            inp = inp + nt(act_ref[:, at + tile : at + 2 * tile], gate_ref[e, :, f : f + tile])
            inp = inp + nt(act_ref[:, at + 2 * tile : at + 3 * tile], up_ref[e, :, f : f + tile])
        outs.append(out)
        ins.append(inp)
    out_ref[:, :width] = jnp.where(first, outs[0], outs[1]).astype(BF)
    out_ref[:, width:] = jnp.where(first, ins[0], ins[1]).astype(BF)


def full(v):
    return pl.BlockSpec(v.shape, lambda i: (0,) * len(v.shape))


TILE = 256


def grant(mib):
    return pltpu.CompilerParams(vmem_limit_bytes=mib * 2**20)


def cost(flops, moved):
    return pl.CostEstimate(flops=flops, bytes_accessed=moved, transcendentals=0)


AFTER = pl.BlockSpec(memory_space=pl.ANY)


def call(kernel, operands, shapes, name, flops, moved, after=(), mib=12):
    shapes = [jax.ShapeDtypeStruct(shape, dtype) for shape, dtype in shapes]
    outs = pl.pallas_call(
        kernel,
        out_shape=shapes,
        grid=(1,),
        in_specs=[full(v) for v in operands] + [AFTER] * len(after),
        out_specs=[full(v) for v in shapes],
        compiler_params=grant(mib),
        cost_estimate=cost(flops, moved),
        name=name,
    )(*operands, *after)
    return outs if len(outs) > 1 else outs[0]


def expand(room, core, halves, other, weights):
    half, wide = other.shape
    ring, cores, share, _ = halves.shape
    width, hidden_units = weights[0].shape[1:]
    gate_spec = pl.BlockSpec((2, width, TILE), lambda j, c: (0, 0, j))
    down_spec = pl.BlockSpec((2, TILE, width), lambda j, c: (0, j, 0))
    return pl.pallas_call(
        lambda *refs: expand_kernel(room, *refs),
        out_shape=jax.ShapeDtypeStruct((half, 3 * hidden_units), BF),
        grid_spec=pltpu.PrefetchScalarGridSpec(
            num_scalar_prefetch=1,
            grid=(hidden_units // TILE,),
            in_specs=[
                pl.BlockSpec((ring, None, share, wide), lambda j, c: (0, c[0], 0, 0)),
                pl.BlockSpec((half, wide), lambda j, c: (0, 0)),
            ]
            + [gate_spec] * 4
            + [down_spec] * 2,
            out_specs=pl.BlockSpec((half, 3 * TILE), lambda j, c: (0, j)),
        ),
        compiler_params=grant(20),
        cost_estimate=cost(2**31, 2**23),
        name="expand",
    )(core.astype(jnp.int32).reshape(1), halves, other, *weights)


def contract(room, acts, weights, after, pieces=2):
    total, wide = acts.shape
    width = weights[0].shape[1]
    whole = lambda w: pl.BlockSpec(w.shape, lambda i: (0, 0, 0))
    return pl.pallas_call(
        lambda *refs: contract_kernel(room, TILE, *refs),
        out_shape=jax.ShapeDtypeStruct((total, 2 * width), BF),
        grid=(pieces,),
        in_specs=[pl.BlockSpec((total // pieces, wide), lambda i: (i, 0))] + [whole(w) for w in weights] + [AFTER],
        out_specs=pl.BlockSpec((total // pieces, 2 * width), lambda i: (i, 0)),
        compiler_params=grant(52),
        cost_estimate=cost(2**31, 2**23),
        name="contract",
    )(acts, *weights, after)


def local(
    hidden_in,
    out_grad,
    routes,
    router_weight,
    expert_bias,
    gate_weight,
    up_weight,
    down_weight,
    lengths,
    advantages,
    plan,
):
    columns = lax.axis_size("expert")
    cores = 2
    ring = lax.axis_size("dp") // cores
    core = lax.rem(lax.axis_index("dp"), cores)
    rings = [[cores * y + c for y in range(ring)] for c in range(cores)]
    swap = [(i, i ^ 1) for i in range(cores * ring)]
    width = hidden_in.shape[2]
    hidden_units = gate_weight.shape[2]
    experts = router_weight.shape[1]
    tokens, tops = hidden_in.shape[1], routes.shape[2]
    room = tokens * tops // experts + 2
    block, total = 2 * room, experts * room
    x, g = hidden_in[0], out_grad[0]
    routes_t = routes[0].T

    def exchange(buffer):
        blocks = buffer.reshape(columns, block, 2 * width)
        return lax.all_to_all(blocks, "expert", split_axis=0, concat_axis=0, tiled=True)

    buffer = call(
        lambda *refs: dispatch_kernel(room, *refs),
        (routes_t, lengths, plan, x, g),
        [((total, 2 * width), BF)],
        "dispatch",
        2**30,
        2**21,
        mib=56,
    )
    arrived = exchange(buffer)
    gate_o = lax.ppermute(gate_weight, "dp", swap)
    up_o = lax.ppermute(up_weight, "dp", swap)
    down_o = lax.ppermute(down_weight, "dp", swap)

    half = columns // cores * block
    halves = arrived.reshape(ring, cores, half // ring, 2 * width)
    yours = lax.dynamic_index_in_dim(halves, 1 - core, 1, keepdims=False).reshape(half, 2 * width)
    other = lax.ppermute(yours, "dp", swap)
    part = expand(room, core, halves, other, (gate_weight, gate_o, up_weight, up_o, down_weight, down_o))
    summed = lax.psum_scatter(part, "dp", scatter_dimension=0, axis_index_groups=rings, tiled=True)

    logit_part = call(
        logits_kernel, (router_weight.T, x), [((experts, tokens), BF)], "logits", 2**23, 2**18, after=(part,)
    )
    logit_parts = lax.all_gather(logit_part, "dp", axis=0)
    counts = jnp.sum(arrived[:, room - 1, :width].astype(F32), axis=0, keepdims=True)
    weighting, token_scale, new_bias = call(
        lambda *refs: home_kernel(room, *refs),
        (routes_t, logit_parts, lengths, advantages, plan, expert_bias[None], counts),
        [((tokens, total), BF), ((tokens, 1), F32), ((1, experts), F32)],
        "home",
        2**28,
        2**21,
    )

    acts = call(
        lambda *refs: activate_kernel(TILE, *refs),
        (summed,),
        [(summed.shape, BF)],
        "activate",
        2**26,
        2**20,
        after=(weighting,),
        mib=60,
    )
    every = lax.all_gather(acts, "dp", axis=0, tiled=True)
    back = exchange(contract(room, every, (gate_weight, up_weight, down_weight), weighting))
    layer_out, input_grad = call(
        combine_kernel,
        (weighting, back.reshape(total, 2 * width), token_scale),
        [((tokens, width), BF)] * 2,
        "combine",
        2**27,
        2**21,
    )
    new_bias = new_bias[0]
    return layer_out[None], input_grad[None], new_bias


def solution(mesh):
    in_specs = (
        P("expert", None, "dp"),
        P("expert", None, "dp"),
        P("expert", None, None),
        P("dp", None),
        P(),
        P("expert", "dp", None),
        P("expert", "dp", None),
        P("expert", None, "dp"),
        P("expert", None),
        P("expert", None),
        P("expert", None),
    )
    out_specs = (P("expert", None, "dp"), P("expert", None, "dp"), P())
    return jax.shard_map(local, mesh=mesh, in_specs=in_specs, out_specs=out_specs, check_vma=False)
```

```python
import jax
import jax.numpy as jnp
from jax import lax
from jax.experimental import pallas as pl
from jax.experimental.pallas import tpu as pltpu
from jax.sharding import PartitionSpec as P

LEARN_GROUPS = 12
HEAD = 8
bias_rate = 0.1
BF = jnp.bfloat16
F32 = jnp.float32


def nn(a, b):
    return lax.dot_general(a, b, (((1,), (0,)), ((), ())), preferred_element_type=F32)


def nt(a, b):
    return lax.dot_general(a, b, (((1,), (1,)), ((), ())), preferred_element_type=F32)


def ranks(routes_t, experts):
    tops, rows = routes_t.shape
    ids = lax.broadcasted_iota(jnp.int32, (experts, rows), 0)
    member = ids == routes_t[0:1, :]
    for k in range(1, tops):
        member = member | (ids == routes_t[k : k + 1, :])
    hot = member.astype(F32).astype(BF)
    earlier = (
        lax.broadcasted_iota(jnp.int32, (rows, rows), 0) < lax.broadcasted_iota(jnp.int32, (rows, rows), 1)
    ).astype(F32).astype(BF)
    place = nn(hot, earlier)
    return hot, jnp.where(member, place, -1.0).astype(BF)


def dispatch_kernel(room, routes_ref, lens_ref, plan_ref, x_ref, g_ref, buf_ref):
    total = buf_ref.shape[0]
    experts = total // room
    rows, width = x_ref.shape
    hot, value = ranks(routes_ref[...], experts)
    row = lax.broadcasted_iota(jnp.int32, (total, experts), 0)
    first = lax.broadcasted_iota(jnp.int32, (total, experts), 1) * room
    spread = ((row >= first) & (row < first + room)).astype(F32).astype(BF)
    wide = nn(spread, value)
    line = lax.broadcasted_iota(jnp.int32, (total, rows), 0)
    select = (wide.astype(jnp.int32) == lax.rem(line, room)).astype(F32).astype(BF)
    loads = nt(jnp.ones((8, rows), BF), hot)[0:1, :]
    group = lax.broadcasted_iota(jnp.int32, (1, width // 2), 1)
    chosen = jnp.zeros((1, width // 2), F32)
    for r in range(plan_ref.shape[1]):
        chosen = chosen + jnp.where(group == plan_ref[:, r : r + 1], lens_ref[:, r : r + 1], 0).astype(F32)
    pad = jnp.zeros((1, width // 2 - experts), F32)
    counts = jnp.concatenate([loads, pad, chosen], axis=1)
    carrier = lax.rem(lax.broadcasted_iota(jnp.int32, (total, width), 0), 2 * room) == room - 1
    sent = nn(select, x_ref[...])
    buf_ref[:, :width] = jnp.where(carrier, jnp.broadcast_to(counts, sent.shape), sent).astype(BF)
    buf_ref[:, width:] = nn(select, g_ref[...]).astype(BF)


def logits_kernel(router_ref, x_ref, after_ref, out_ref):
    out_ref[...] = nt(router_ref[...], x_ref[...]).astype(BF)


def expand_kernel(room, core_ref, own_ref, oth_ref, go_ref, gx_ref, uo_ref, ux_ref, do_ref, dx_ref, out_ref):
    rows = oth_ref.shape[0]
    width = oth_ref.shape[1] // 2
    tile = go_ref.shape[2]
    own_x = own_ref[:, :, :width].reshape(rows, width)
    own_g = own_ref[:, :, width:].reshape(rows, width)
    oth_x, oth_g = oth_ref[:, :width], oth_ref[:, width:]
    first = lax.rem(lax.broadcasted_iota(jnp.int32, (rows, tile), 0), 2 * room) < room
    gate = [nn(own_x, go_ref[e]) + nn(oth_x, gx_ref[e]) for e in range(2)]
    out_ref[:, :tile] = jnp.where(first, gate[0], gate[1]).astype(BF)
    up = [nn(own_x, uo_ref[e]) + nn(oth_x, ux_ref[e]) for e in range(2)]
    out_ref[:, tile : 2 * tile] = jnp.where(first, up[0], up[1]).astype(BF)
    back = [nt(own_g, do_ref[e]) + nt(oth_g, dx_ref[e]) for e in range(2)]
    out_ref[:, 2 * tile :] = jnp.where(first, back[0], back[1]).astype(BF)


def home_kernel(
    room, routes_ref, logits_ref, lens_ref, adv_ref, plan_ref, bias_ref, counts_ref, head_ref, tail_ref, scale_ref, new_ref
):
    tokens, total = head_ref.shape[0], head_ref.shape[1] + tail_ref.shape[1]
    experts = total // room
    hot, value = ranks(routes_ref[...], experts)
    logits = logits_ref[0].astype(F32)
    for m in range(1, logits_ref.shape[0]):
        logits = logits + logits_ref[m].astype(F32)
    scores = jax.nn.sigmoid(logits) * hot.astype(F32)
    mixing = (scores / jnp.sum(scores, axis=0, keepdims=True)).astype(BF)
    row = lax.broadcasted_iota(jnp.int32, (total, experts), 0)
    begin = lax.broadcasted_iota(jnp.int32, (total, experts), 1) * room
    spread = ((row >= begin) & (row < begin + room)).astype(F32).astype(BF)
    line = lax.rem(lax.broadcasted_iota(jnp.int32, (total, tokens), 0), room)
    landing = nn(spread, value).astype(jnp.int32) == line
    weight = jnp.where(landing, nn(spread, mixing), 0.0).reshape(-1, 2 * room, tokens)
    head_ref[...] = weight[:, :HEAD].reshape(-1, tokens).T.astype(BF)
    tail_ref[...] = weight[:, HEAD:].reshape(-1, tokens).T.astype(BF)
    half = counts_ref.shape[1] // 2
    groups = counts_ref[:, half:]
    group = lax.broadcasted_iota(jnp.int32, (1, half), 1)
    token = lax.broadcasted_iota(jnp.int32, (tokens, 1), 0)
    mean = experts // 2 * tokens / LEARN_GROUPS
    start, scale = jnp.zeros((1, 1), jnp.int32), jnp.zeros((tokens, 1), F32)
    for r in range(plan_ref.shape[1]):
        end = start + lens_ref[:, r : r + 1]
        size = jnp.sum(jnp.where(group == plan_ref[:, r : r + 1], groups, 0.0), axis=1, keepdims=True)
        scale = jnp.where((token >= start) & (token < end), adv_ref[:, r : r + 1] * mean / size, scale)
        start = end
    scale_ref[...] = scale
    load = routes_ref.shape[0] * experts // 2 * tokens / experts
    new_ref[...] = bias_ref[...] + bias_rate * (1.0 - counts_ref[:, :experts] / load)


def activate(gate, up, back):
    s = jax.nn.sigmoid(gate)
    swish = gate * s
    return swish * up, back * up * s * (1.0 + gate * (1.0 - s)), back * swish


def activate_kernel(tile, block, low, high, in_ref, after_ref, out_ref):
    for at in range(0, in_ref.shape[1], 3 * tile):
        parts = []
        for i in range(3):
            part = in_ref[:, at + tile * i : at + tile * (i + 1)].astype(F32).reshape(-1, block, tile)
            parts.append(part[:, low:high].reshape(-1, tile))
        for i, value in enumerate(activate(*parts)):
            out_ref[:, at + tile * i : at + tile * (i + 1)] = value.astype(BF)


def combine_kernel(head_ref, tail_ref, back_head_ref, back_tail_ref, scale_ref, out_ref, grad_ref):
    width = out_ref.shape[1]
    head, tail = head_ref[...], tail_ref[...]
    out_ref[...] = (nn(head, back_head_ref[:, :width]) + nn(tail, back_tail_ref[:, :width])).astype(BF)
    grad = nn(head, back_head_ref[:, width:]) + nn(tail, back_tail_ref[:, width:])
    grad_ref[...] = (scale_ref[...] * grad).astype(BF)


def contract_kernel(block, first_rows, tile, act_ref, gate_ref, up_ref, down_ref, after_ref, out_ref):
    rows, width = act_ref.shape[0], gate_ref.shape[1]
    outs, ins = [], []
    for e in range(1 if first_rows == block else 2):
        out, inp = jnp.zeros((rows, width), F32), jnp.zeros((rows, width), F32)
        for j in range(gate_ref.shape[2] // tile):
            at, f = 3 * tile * j, tile * j
            out = out + nn(act_ref[:, at : at + tile], down_ref[e, f : f + tile, :])
            inp = inp + nt(act_ref[:, at + tile : at + 2 * tile], gate_ref[e, :, f : f + tile])
            inp = inp + nt(act_ref[:, at + 2 * tile : at + 3 * tile], up_ref[e, :, f : f + tile])
        outs.append(out)
        ins.append(inp)
    if first_rows < block:
        first = lax.rem(lax.broadcasted_iota(jnp.int32, (rows, width), 0), block) < first_rows
        outs[0] = jnp.where(first, outs[0], outs[1])
        ins[0] = jnp.where(first, ins[0], ins[1])
    out_ref[:, :width] = outs[0].astype(BF)
    out_ref[:, width:] = ins[0].astype(BF)


def full(v):
    return pl.BlockSpec(v.shape, lambda i: (0,) * len(v.shape))


TILE = 256


def grant(mib):
    return pltpu.CompilerParams(vmem_limit_bytes=mib * 2**20)


def cost(flops, moved):
    return pl.CostEstimate(flops=flops, bytes_accessed=moved, transcendentals=0)


AFTER = pl.BlockSpec(memory_space=pl.ANY)


def call(kernel, operands, shapes, name, flops, moved, after=(), mib=12):
    shapes = [jax.ShapeDtypeStruct(shape, dtype) for shape, dtype in shapes]
    outs = pl.pallas_call(
        kernel,
        out_shape=shapes,
        grid=(1,),
        in_specs=[full(v) for v in operands] + [AFTER] * len(after),
        out_specs=[full(v) for v in shapes],
        compiler_params=grant(mib),
        cost_estimate=cost(flops, moved),
        name=name,
    )(*operands, *after)
    return outs if len(outs) > 1 else outs[0]


def expand(room, core, halves, other, weights):
    half, wide = other.shape
    ring, cores, share, _ = halves.shape
    width, hidden_units = weights[0].shape[1:]
    gate_spec = pl.BlockSpec((2, width, TILE), lambda j, c: (0, 0, j))
    down_spec = pl.BlockSpec((2, TILE, width), lambda j, c: (0, j, 0))
    return pl.pallas_call(
        lambda *refs: expand_kernel(room, *refs),
        out_shape=jax.ShapeDtypeStruct((half, 3 * hidden_units), BF),
        grid_spec=pltpu.PrefetchScalarGridSpec(
            num_scalar_prefetch=1,
            grid=(hidden_units // TILE,),
            in_specs=[
                pl.BlockSpec((ring, None, share, wide), lambda j, c: (0, c[0], 0, 0)),
                pl.BlockSpec((half, wide), lambda j, c: (0, 0)),
            ]
            + [gate_spec] * 4
            + [down_spec] * 2,
            out_specs=pl.BlockSpec((half, 3 * TILE), lambda j, c: (0, j)),
        ),
        compiler_params=grant(20),
        cost_estimate=cost(2**31, 2**23),
        name="expand",
    )(core.astype(jnp.int32).reshape(1), halves, other, *weights)


def contract(block, first_rows, acts, weights, after, pieces):
    total, wide = acts.shape
    width = weights[0].shape[1]
    whole = lambda w: pl.BlockSpec(w.shape, lambda i: (0, 0, 0))
    return pl.pallas_call(
        lambda *refs: contract_kernel(block, first_rows, TILE, *refs),
        out_shape=jax.ShapeDtypeStruct((total, 2 * width), BF),
        grid=(pieces,),
        in_specs=[pl.BlockSpec((total // pieces, wide), lambda i: (i, 0))] + [whole(w) for w in weights] + [AFTER],
        out_specs=pl.BlockSpec((total // pieces, 2 * width), lambda i: (i, 0)),
        compiler_params=grant(48),
        cost_estimate=cost(2**31, 2**23),
        name="contract",
    )(acts, *weights, after)


def local(
    hidden_in,
    out_grad,
    routes,
    router_weight,
    expert_bias,
    gate_weight,
    up_weight,
    down_weight,
    lengths,
    advantages,
    plan,
):
    columns = lax.axis_size("expert")
    cores = 2
    ring = lax.axis_size("dp") // cores
    core = lax.rem(lax.axis_index("dp"), cores)
    rings = [[cores * y + c for y in range(ring)] for c in range(cores)]
    swap = [(i, i ^ 1) for i in range(cores * ring)]
    width = hidden_in.shape[2]
    hidden_units = gate_weight.shape[2]
    experts = router_weight.shape[1]
    tokens, tops = hidden_in.shape[1], routes.shape[2]
    room = tokens * tops // experts + 2
    block, total = 2 * room, experts * room
    x, g = hidden_in[0], out_grad[0]
    routes_t = routes[0].T

    def exchange(buffer):
        blocks = buffer.reshape(columns, -1, 2 * width)
        return lax.all_to_all(blocks, "expert", split_axis=0, concat_axis=0, tiled=True)

    buffer = call(
        lambda *refs: dispatch_kernel(room, *refs),
        (routes_t, lengths, plan, x, g),
        [((total, 2 * width), BF)],
        "dispatch",
        2**30,
        2**21,
        mib=56,
    )
    arrived = exchange(buffer)
    gate_o = lax.ppermute(gate_weight, "dp", swap)
    up_o = lax.ppermute(up_weight, "dp", swap)
    down_o = lax.ppermute(down_weight, "dp", swap)

    half = columns // cores * block
    halves = arrived.reshape(ring, cores, half // ring, 2 * width)
    yours = lax.dynamic_index_in_dim(halves, 1 - core, 1, keepdims=False).reshape(half, 2 * width)
    other = lax.ppermute(yours, "dp", swap)
    part = expand(room, core, halves, other, (gate_weight, gate_o, up_weight, up_o, down_weight, down_o))
    summed = lax.psum_scatter(part, "dp", scatter_dimension=0, axis_index_groups=rings, tiled=True)

    logit_part = call(
        logits_kernel, (router_weight.T, x), [((experts, tokens), BF)], "logits", 2**23, 2**18, after=(part,)
    )
    logit_parts = lax.all_gather(logit_part, "dp", axis=0)
    counts = jnp.sum(arrived[:, room - 1, :width].astype(F32), axis=0, keepdims=True)
    head, tail, token_scale, new_bias = call(
        lambda *refs: home_kernel(room, *refs),
        (routes_t, logit_parts, lengths, advantages, plan, expert_bias[None], counts),
        [
            ((tokens, columns * HEAD), BF),
            ((tokens, columns * (block - HEAD)), BF),
            ((tokens, 1), F32),
            ((1, experts), F32),
        ],
        "home",
        2**28,
        2**21,
    )

    share = summed.shape[0] // block

    def act(low, high, after):
        return call(
            lambda *refs: activate_kernel(TILE, block, low, high, *refs),
            (summed,),
            [((share * (high - low), 3 * hidden_units), BF)],
            "activate",
            2**26,
            2**20,
            after=(after,),
            mib=60,
        )

    own = (gate_weight, up_weight, down_weight)
    acts_head = act(0, HEAD, tail)
    acts_tail = act(HEAD, block, acts_head)
    every_head = lax.all_gather(acts_head, "dp", axis=0, tiled=True)
    every_tail = lax.all_gather(acts_tail, "dp", axis=0, tiled=True)
    results_head = contract(HEAD, HEAD, every_head, own, tail, 1)
    back_head = exchange(results_head)
    back_tail = exchange(contract(block - HEAD, room - HEAD, every_tail, own, results_head, 2))
    layer_out, input_grad = call(
        combine_kernel,
        (head, tail, back_head.reshape(-1, 2 * width), back_tail.reshape(-1, 2 * width), token_scale),
        [((tokens, width), BF)] * 2,
        "combine",
        2**27,
        2**21,
    )
    new_bias = new_bias[0]
    return layer_out[None], input_grad[None], new_bias


def solution(mesh):
    in_specs = (
        P("expert", None, "dp"),
        P("expert", None, "dp"),
        P("expert", None, None),
        P("dp", None),
        P(),
        P("expert", "dp", None),
        P("expert", "dp", None),
        P("expert", None, "dp"),
        P("expert", None),
        P("expert", None),
        P("expert", None),
    )
    out_specs = (P("expert", None, "dp"), P("expert", None, "dp"), P())
    return jax.shard_map(local, mesh=mesh, in_specs=in_specs, out_specs=out_specs, check_vma=False)
```

```python
import jax
import jax.numpy as jnp
from jax import lax
from jax.experimental import pallas as pl
from jax.experimental.pallas import tpu as pltpu
from jax.sharding import PartitionSpec as P

LEARN_GROUPS = 12
bias_rate = 0.1
BF = jnp.bfloat16
F32 = jnp.float32


def nn(a, b):
    return lax.dot_general(a, b, (((1,), (0,)), ((), ())), preferred_element_type=F32)


def nt(a, b):
    return lax.dot_general(a, b, (((1,), (1,)), ((), ())), preferred_element_type=F32)


def ranks(routes_t, experts):
    tops, rows = routes_t.shape
    ids = lax.broadcasted_iota(jnp.int32, (experts, rows), 0)
    member = ids == routes_t[0:1, :]
    for k in range(1, tops):
        member = member | (ids == routes_t[k : k + 1, :])
    hot = member.astype(F32).astype(BF)
    earlier = (
        lax.broadcasted_iota(jnp.int32, (rows, rows), 0) < lax.broadcasted_iota(jnp.int32, (rows, rows), 1)
    ).astype(F32).astype(BF)
    place = nn(hot, earlier)
    return hot, jnp.where(member, place, -1.0).astype(BF)


def dispatch_kernel(room, routes_ref, lens_ref, plan_ref, x_ref, g_ref, buf_ref):
    total = buf_ref.shape[0]
    experts = total // room
    rows, width = x_ref.shape
    hot, value = ranks(routes_ref[...], experts)
    row = lax.broadcasted_iota(jnp.int32, (total, experts), 0)
    first = lax.broadcasted_iota(jnp.int32, (total, experts), 1) * room
    spread = ((row >= first) & (row < first + room)).astype(F32).astype(BF)
    wide = nn(spread, value)
    line = lax.broadcasted_iota(jnp.int32, (total, rows), 0)
    select = (wide.astype(jnp.int32) == lax.rem(line, room)).astype(F32).astype(BF)
    loads = nt(jnp.ones((8, rows), BF), hot)[0:1, :]
    group = lax.broadcasted_iota(jnp.int32, (1, width // 2), 1)
    chosen = jnp.zeros((1, width // 2), F32)
    for r in range(plan_ref.shape[1]):
        chosen = chosen + jnp.where(group == plan_ref[:, r : r + 1], lens_ref[:, r : r + 1], 0).astype(F32)
    pad = jnp.zeros((1, width // 2 - experts), F32)
    counts = jnp.concatenate([loads, pad, chosen], axis=1)
    carrier = lax.rem(lax.broadcasted_iota(jnp.int32, (total, width), 0), 2 * room) == room - 1
    sent = nn(select, x_ref[...])
    buf_ref[:, :width] = jnp.where(carrier, jnp.broadcast_to(counts, sent.shape), sent).astype(BF)
    buf_ref[:, width:] = nn(select, g_ref[...]).astype(BF)


def logits_kernel(router_ref, x_ref, after_ref, out_ref):
    out_ref[...] = nt(router_ref[...], x_ref[...]).astype(BF)


def expand_kernel(room, core_ref, own_ref, oth_ref, go_ref, gx_ref, uo_ref, ux_ref, do_ref, dx_ref, out_ref):
    rows = oth_ref.shape[0]
    width = oth_ref.shape[1] // 2
    tile = go_ref.shape[2]
    own_x = own_ref[:, :, :width].reshape(rows, width)
    own_g = own_ref[:, :, width:].reshape(rows, width)
    oth_x, oth_g = oth_ref[:, :width], oth_ref[:, width:]
    first = lax.rem(lax.broadcasted_iota(jnp.int32, (rows, tile), 0), 2 * room) < room
    gate = [nn(own_x, go_ref[e]) + nn(oth_x, gx_ref[e]) for e in range(2)]
    out_ref[:, :tile] = jnp.where(first, gate[0], gate[1]).astype(BF)
    up = [nn(own_x, uo_ref[e]) + nn(oth_x, ux_ref[e]) for e in range(2)]
    out_ref[:, tile : 2 * tile] = jnp.where(first, up[0], up[1]).astype(BF)
    back = [nt(own_g, do_ref[e]) + nt(oth_g, dx_ref[e]) for e in range(2)]
    out_ref[:, 2 * tile :] = jnp.where(first, back[0], back[1]).astype(BF)


def home_kernel(
    room, routes_ref, logits_ref, lens_ref, adv_ref, plan_ref, bias_ref, counts_ref, weight_ref, scale_ref, new_ref
):
    tokens, total = weight_ref.shape
    experts = total // room
    hot, value = ranks(routes_ref[...], experts)
    logits = logits_ref[0].astype(F32)
    for m in range(1, logits_ref.shape[0]):
        logits = logits + logits_ref[m].astype(F32)
    scores = jax.nn.sigmoid(logits) * hot.astype(F32)
    mixing = (scores / jnp.sum(scores, axis=0, keepdims=True)).astype(BF)
    row = lax.broadcasted_iota(jnp.int32, (total, experts), 0)
    begin = lax.broadcasted_iota(jnp.int32, (total, experts), 1) * room
    spread = ((row >= begin) & (row < begin + room)).astype(F32).astype(BF)
    line = lax.rem(lax.broadcasted_iota(jnp.int32, (total, tokens), 0), room)
    landing = nn(spread, value).astype(jnp.int32) == line
    weight_ref[...] = jnp.where(landing, nn(spread, mixing), 0.0).T.astype(BF)
    half = counts_ref.shape[1] // 2
    groups = counts_ref[:, half:]
    group = lax.broadcasted_iota(jnp.int32, (1, half), 1)
    token = lax.broadcasted_iota(jnp.int32, (tokens, 1), 0)
    mean = experts // 2 * tokens / LEARN_GROUPS
    start, scale = jnp.zeros((1, 1), jnp.int32), jnp.zeros((tokens, 1), F32)
    for r in range(plan_ref.shape[1]):
        end = start + lens_ref[:, r : r + 1]
        size = jnp.sum(jnp.where(group == plan_ref[:, r : r + 1], groups, 0.0), axis=1, keepdims=True)
        scale = jnp.where((token >= start) & (token < end), adv_ref[:, r : r + 1] * mean / size, scale)
        start = end
    scale_ref[...] = scale
    load = routes_ref.shape[0] * experts // 2 * tokens / experts
    new_ref[...] = bias_ref[...] + bias_rate * (1.0 - counts_ref[:, :experts] / load)


def activate(gate, up, back):
    s = jax.nn.sigmoid(gate)
    swish = gate * s
    return swish * up, back * up * s * (1.0 + gate * (1.0 - s)), back * swish


def activate_kernel(tile, in_ref, after_ref, out_ref):
    for at in range(0, in_ref.shape[1], 3 * tile):
        parts = [in_ref[:, at + tile * i : at + tile * (i + 1)].astype(F32) for i in range(3)]
        for i, value in enumerate(activate(*parts)):
            out_ref[:, at + tile * i : at + tile * (i + 1)] = value.astype(BF)


def combine_kernel(weight_ref, back_ref, scale_ref, out_ref, grad_ref):
    width = out_ref.shape[1]
    out_ref[...] = nn(weight_ref[...], back_ref[:, :width]).astype(BF)
    grad_ref[...] = (scale_ref[...] * nn(weight_ref[...], back_ref[:, width:])).astype(BF)


def contract_kernel(room, tile, act_ref, gate_ref, up_ref, down_ref, after_ref, out_ref):
    rows, width = act_ref.shape[0], gate_ref.shape[1]
    first = lax.rem(lax.broadcasted_iota(jnp.int32, (rows, width), 0), 2 * room) < room
    outs, ins = [], []
    for e in range(2):
        out, inp = jnp.zeros((rows, width), F32), jnp.zeros((rows, width), F32)
        for j in range(gate_ref.shape[2] // tile):
            at, f = 3 * tile * j, tile * j
            out = out + nn(act_ref[:, at : at + tile], down_ref[e, f : f + tile, :])
            inp = inp + nt(act_ref[:, at + tile : at + 2 * tile], gate_ref[e, :, f : f + tile])
            inp = inp + nt(act_ref[:, at + 2 * tile : at + 3 * tile], up_ref[e, :, f : f + tile])
        outs.append(out)
        ins.append(inp)
    out_ref[:, :width] = jnp.where(first, outs[0], outs[1]).astype(BF)
    out_ref[:, width:] = jnp.where(first, ins[0], ins[1]).astype(BF)


def full(v):
    return pl.BlockSpec(v.shape, lambda i: (0,) * len(v.shape))


TILE = 256


def grant(mib):
    return pltpu.CompilerParams(vmem_limit_bytes=mib * 2**20)


def cost(flops, moved):
    return pl.CostEstimate(flops=flops, bytes_accessed=moved, transcendentals=0)


AFTER = pl.BlockSpec(memory_space=pl.ANY)


def call(kernel, operands, shapes, name, flops, moved, after=(), mib=12):
    shapes = [jax.ShapeDtypeStruct(shape, dtype) for shape, dtype in shapes]
    outs = pl.pallas_call(
        kernel,
        out_shape=shapes,
        grid=(1,),
        in_specs=[full(v) for v in operands] + [AFTER] * len(after),
        out_specs=[full(v) for v in shapes],
        compiler_params=grant(mib),
        cost_estimate=cost(flops, moved),
        name=name,
    )(*operands, *after)
    return outs if len(outs) > 1 else outs[0]


def expand(room, core, halves, other, weights):
    half, wide = other.shape
    ring, cores, share, _ = halves.shape
    width, hidden_units = weights[0].shape[1:]
    gate_spec = pl.BlockSpec((2, width, TILE), lambda j, c: (0, 0, j))
    down_spec = pl.BlockSpec((2, TILE, width), lambda j, c: (0, j, 0))
    return pl.pallas_call(
        lambda *refs: expand_kernel(room, *refs),
        out_shape=jax.ShapeDtypeStruct((half, 3 * hidden_units), BF),
        grid_spec=pltpu.PrefetchScalarGridSpec(
            num_scalar_prefetch=1,
            grid=(hidden_units // TILE,),
            in_specs=[
                pl.BlockSpec((ring, None, share, wide), lambda j, c: (0, c[0], 0, 0)),
                pl.BlockSpec((half, wide), lambda j, c: (0, 0)),
            ]
            + [gate_spec] * 4
            + [down_spec] * 2,
            out_specs=pl.BlockSpec((half, 3 * TILE), lambda j, c: (0, j)),
        ),
        compiler_params=grant(20),
        cost_estimate=cost(2**31, 2**23),
        name="expand",
    )(core.astype(jnp.int32).reshape(1), halves, other, *weights)


def contract(room, acts, weights, after, pieces=3):
    total, wide = acts.shape
    width = weights[0].shape[1]
    whole = lambda w: pl.BlockSpec(w.shape, lambda i: (0, 0, 0))
    return pl.pallas_call(
        lambda *refs: contract_kernel(room, TILE, *refs),
        out_shape=jax.ShapeDtypeStruct((total, 2 * width), BF),
        grid=(pieces,),
        in_specs=[pl.BlockSpec((total // pieces, wide), lambda i: (i, 0))] + [whole(w) for w in weights] + [AFTER],
        out_specs=pl.BlockSpec((total // pieces, 2 * width), lambda i: (i, 0)),
        compiler_params=grant(48),
        cost_estimate=cost(2**31, 2**23),
        name="contract",
    )(acts, *weights, after)


def local(
    hidden_in,
    out_grad,
    routes,
    router_weight,
    expert_bias,
    gate_weight,
    up_weight,
    down_weight,
    lengths,
    advantages,
    plan,
):
    columns = lax.axis_size("expert")
    cores = 2
    ring = lax.axis_size("dp") // cores
    core = lax.rem(lax.axis_index("dp"), cores)
    rings = [[cores * y + c for y in range(ring)] for c in range(cores)]
    swap = [(i, i ^ 1) for i in range(cores * ring)]
    width = hidden_in.shape[2]
    hidden_units = gate_weight.shape[2]
    experts = router_weight.shape[1]
    tokens, tops = hidden_in.shape[1], routes.shape[2]
    room = tokens * tops // experts + 2
    block, total = 2 * room, experts * room
    x, g = hidden_in[0], out_grad[0]
    routes_t = routes[0].T

    def exchange(buffer):
        blocks = buffer.reshape(columns, block, 2 * width)
        return lax.all_to_all(blocks, "expert", split_axis=0, concat_axis=0, tiled=True)

    buffer = call(
        lambda *refs: dispatch_kernel(room, *refs),
        (routes_t, lengths, plan, x, g),
        [((total, 2 * width), BF)],
        "dispatch",
        2**30,
        2**21,
        mib=56,
    )
    arrived = exchange(buffer)
    gate_o = lax.ppermute(gate_weight, "dp", swap)
    up_o = lax.ppermute(up_weight, "dp", swap)
    down_o = lax.ppermute(down_weight, "dp", swap)

    half = columns // cores * block
    halves = arrived.reshape(ring, cores, half // ring, 2 * width)
    yours = lax.dynamic_index_in_dim(halves, 1 - core, 1, keepdims=False).reshape(half, 2 * width)
    other = lax.ppermute(yours, "dp", swap)
    part = expand(room, core, halves, other, (gate_weight, gate_o, up_weight, up_o, down_weight, down_o))
    summed = lax.psum_scatter(part, "dp", scatter_dimension=0, axis_index_groups=rings, tiled=True)

    logit_part = call(
        logits_kernel, (router_weight.T, x), [((experts, tokens), BF)], "logits", 2**23, 2**18, after=(part,)
    )
    logit_parts = lax.all_gather(logit_part, "dp", axis=0)
    counts = jnp.sum(arrived[:, room - 1, :width].astype(F32), axis=0, keepdims=True)
    weighting, token_scale, new_bias = call(
        lambda *refs: home_kernel(room, *refs),
        (routes_t, logit_parts, lengths, advantages, plan, expert_bias[None], counts),
        [((tokens, total), BF), ((tokens, 1), F32), ((1, experts), F32)],
        "home",
        2**28,
        2**21,
    )

    acts = call(
        lambda *refs: activate_kernel(TILE, *refs),
        (summed,),
        [(summed.shape, BF)],
        "activate",
        2**26,
        2**20,
        after=(weighting,),
        mib=60,
    )
    every = lax.all_gather(acts, "dp", axis=0, tiled=True)
    back = exchange(contract(room, every, (gate_weight, up_weight, down_weight), weighting))
    layer_out, input_grad = call(
        combine_kernel,
        (weighting, back.reshape(total, 2 * width), token_scale),
        [((tokens, width), BF)] * 2,
        "combine",
        2**27,
        2**21,
    )
    new_bias = new_bias[0]
    return layer_out[None], input_grad[None], new_bias


def solution(mesh):
    in_specs = (
        P("expert", None, "dp"),
        P("expert", None, "dp"),
        P("expert", None, None),
        P("dp", None),
        P(),
        P("expert", "dp", None),
        P("expert", "dp", None),
        P("expert", None, "dp"),
        P("expert", None),
        P("expert", None),
        P("expert", None),
    )
    out_specs = (P("expert", None, "dp"), P("expert", None, "dp"), P())
    return jax.shard_map(local, mesh=mesh, in_specs=in_specs, out_specs=out_specs, check_vma=False)
```
